128 devices in a mesh: dp: 8 (over x, core), mp: 16 (over y, z).
Axes of the slice: x: 4, y: 4, z: 4, core: 2. Of those that a mesh axis runs over, the one named last changes fastest.
Arguments:
- patches: bfloat16 [3072, 6144], P('dp', 'mp'), may hold values from -6 to 6
- keep_index: int32 [64, 48], P('dp'), may hold values from 0 to 47, each once within a row
- keep_count: int32 [64], replicated, may hold values from 1 to 48, as said below
- pack_dest: int32 [64], replicated, may hold values from 0 to 7, as said below
- pack_offset: int32 [64], replicated, may hold values from 0 to 336, as said below
- w_qkv: bfloat16 [6144, 12288], P(None, 'mp'), may hold values from -0.108253175 to 0.108253175
- q_gain: float32 [128], replicated, may hold values from 0.6 to 5
- k_gain: float32 [128], replicated, may hold values from 0.6 to 5
- w_out: bfloat16 [6144, 4096], P(None, 'mp'), may hold values from -0.09375 to 0.09375
- cotangent: bfloat16 [3072, 6144], P('dp', 'mp'), may hold values from -6 to 6
Outputs:
- block_out: bfloat16 [3072, 6144], P('dp', 'mp')
- patch_grad: bfloat16 [3072, 6144], P('dp', 'mp')
- qkv_grad: float32 [6144, 12288], P('dp', 'mp')
- out_grad: float32 [6144, 4096], P('dp', 'mp')
The draws below stay inside these ranges and needn't reach their ends.
Inputs may be any that keep to these rules, and one draw needn't show every extreme that they name: `pack_dest`: the 8 images s*8 to s*8 + 7 of loader shard s go to 8 different sequences, so every sequence receives exactly one image from each shard. `keep_count`: in every draw all images of some sequence keep all 48 slots. `pack_offset`: the images of one sequence lie back to back from row 0, in some order of their shards; rows after them are padding.
All inputs are finite; a program needn't handle non-finite values.
Results may differ from the reference program's by a relative error of at most 0.02.
The reference program's roundings to bfloat16 on the way count: a program that leaves them out, or rounds other values in their place, can miss the bound.
Values may be sent and summed in bfloat16 or wider, within the bound.
A program may use at most 128 MiB of HBM per device.

```python
import jax
import jax.numpy as jnp
from jax import lax

D = 6144
HEADS = 32
HEAD_DIM = 128
TOK_DEV = 384
PATCHES = 48
IMAGES = 64
TOKENS = 3072
WIDTH = 4096
N_DP = 8
N_MP = 16


def shuffled_rows(key):
    subkeys = jax.random.split(key, N_DP)
    return jax.vmap(lambda subkey: jax.random.permutation(subkey, N_DP))(subkeys).astype(jnp.int32)


def packing(key):
    key_dest, key_count, key_full, key_order = jax.random.split(key, 4)
    destination = shuffled_rows(key_dest)
    counts = jax.random.randint(key_count, (N_DP, N_DP), max(1, PATCHES // 4), PATCHES + 1).astype(jnp.int32)
    full_sequence = jax.random.randint(key_full, (), 0, N_DP).astype(jnp.int32)
    counts = jnp.where(destination == full_sequence, PATCHES, counts).astype(jnp.int32)
    ordering = shuffled_rows(key_order)
    places = jnp.arange(N_DP, dtype=jnp.int32)
    ranking = jnp.sum(jnp.where(ordering[:, :, None] == places[None, None, :], places[None, :, None], 0), axis=1)
    count_by = jnp.sum(jnp.where(destination[None, :, :] == places[:, None, None], counts[None, :, :], 0), axis=2)
    earlier = ranking[:, None, :] < ranking[:, :, None]
    offset_by = jnp.sum(jnp.where(earlier, count_by[:, None, :], 0), axis=2)
    offsets = jnp.sum(jnp.where(destination[:, :, None] == places[None, None, :], offset_by.T[:, None, :], 0), axis=2)
    return (destination.reshape(-1), counts.reshape(-1), offsets.reshape(-1).astype(jnp.int32))


def draw_keep_count(key, part):
    return packing(key)[1]


def draw_pack_dest(key, part):
    return packing(key)[0]


def draw_pack_offset(key, part):
    return packing(key)[2]


def draw_patches(key, part):
    key = jax.random.fold_in(key, 21)
    key_base = jax.random.fold_in(key, 0)
    base = jax.random.normal(key_base, (TOKENS, D), jnp.float32)
    return jnp.clip(base, -6.0, 6.0).astype(jnp.bfloat16)


def draw_w_qkv(key, part):
    key = jax.random.fold_in(key, 22)
    key_base = jax.random.fold_in(key, 0)
    base = jax.random.normal(key_base, (D, HEADS, 3, HEAD_DIM), jnp.float32)
    weights = base * D ** (-0.5)
    limit = 6.0 * (D // 2) ** (-0.5)
    return jnp.clip(weights, -limit, limit).reshape(D, 3 * HEADS * HEAD_DIM).astype(jnp.bfloat16)


def gain_draw(key):
    return jax.random.uniform(key, (HEAD_DIM,), jnp.float32, 0.6, 1.8)


def draw_q_gain(key, part):
    key = jax.random.fold_in(key, 11)
    return gain_draw(key)


def draw_k_gain(key, part):
    key = jax.random.fold_in(key, 12)
    return gain_draw(key)


def block_levels(stream_key, extent, cuts, least, high):
    level = 1.0
    for dim, shards_of in cuts:
        steps = jax.random.uniform(jax.random.fold_in(jax.random.fold_in(stream_key, 6), dim), (shards_of,), jnp.float32, least / len(cuts), high / len(cuts))
        level = level * jnp.repeat(jnp.exp(steps), extent[dim] // shards_of).reshape((-1,) + (1,) * (len(extent) - 1 - dim))
    return level


def normal_values(own_key, extent, deviation, most, cuts=(), kind=jnp.bfloat16):
    entries = deviation * jax.random.normal(own_key, extent, jnp.float32)
    if cuts:
        entries = entries * block_levels(own_key, extent, cuts, -0.22, 0.18)
    return jnp.clip(entries, -most, most).astype(kind)


def setup_inputs(seed: int = 0) -> dict:
    key_of = jax.random.split(jax.random.key(seed), 11)
    return {
        "patches": draw_patches(jax.random.fold_in(key_of[10], 71), 0),
        "keep_index": jax.vmap(lambda own: jax.random.permutation(own, PATCHES))(jax.random.split(key_of[1], IMAGES)).reshape((IMAGES, PATCHES)).astype(jnp.int32),
        "keep_count": draw_keep_count(jax.random.fold_in(key_of[10], 71), 0),
        "pack_dest": draw_pack_dest(jax.random.fold_in(key_of[10], 71), 0),
        "pack_offset": draw_pack_offset(jax.random.fold_in(key_of[10], 71), 0),
        "w_qkv": draw_w_qkv(jax.random.fold_in(key_of[10], 71), 0),
        "q_gain": draw_q_gain(jax.random.fold_in(key_of[10], 71), 0),
        "k_gain": draw_k_gain(jax.random.fold_in(key_of[10], 71), 0),
        "w_out": normal_values(key_of[8], (D, WIDTH), WIDTH ** -0.5, 0.09375, ((1, 16),)),
        "cotangent": normal_values(key_of[9], (TOKENS, D), 1.0, 6.0, ((0, 8), (1, 16))),
    }


EPSILON = 1e-06

def head_norm(values, gain):
    row_mean = lax.optimization_barrier(jnp.mean(values, axis=-1, keepdims=True))
    centred = values - row_mean
    variance = lax.optimization_barrier(jnp.mean(centred * centred, axis=-1, keepdims=True))
    inverse = lax.rsqrt(variance + EPSILON)
    normed = centred * inverse
    return (normed * gain, normed, inverse)

def head_norm_back(incoming, normed, inverse, gain):
    scaled = incoming * gain
    return (scaled - lax.optimization_barrier(jnp.mean(scaled, axis=-1, keepdims=True)) - normed * lax.optimization_barrier(jnp.mean(scaled * normed, axis=-1, keepdims=True))) * inverse

def batched(form, left, right):
    return jnp.einsum(form, left.astype(jnp.float32), right.astype(jnp.float32))

def attention_pass(projected, segment, q_gain, k_gain, grad_attended):
    row_count = projected.shape[0]
    head_count = projected.shape[1]
    head_size = projected.shape[3]
    queries = jnp.swapaxes(projected[:, :, 0, :], 0, 1).astype(jnp.float32)
    keys_raw = jnp.swapaxes(projected[:, :, 1, :], 0, 1).astype(jnp.float32)
    values = jnp.swapaxes(projected[:, :, 2, :], 0, 1)
    query_n, query_hat, query_inv = head_norm(queries, q_gain)
    key_n, key_hat, key_inv = head_norm(keys_raw, k_gain)
    query_b = query_n.astype(jnp.bfloat16)
    key_b = key_n.astype(jnp.bfloat16)
    score_scale = head_size ** (-0.5)
    scores = batched('htd,hsd->hts', query_b, key_b) * score_scale
    allowed = segment[:, None] == segment[None, :]
    scores = jnp.where(allowed[None], scores, -jnp.inf)
    largest = lax.optimization_barrier(jnp.max(scores, axis=-1, keepdims=True))
    exponent = jnp.exp(scores - largest)
    probs = exponent / lax.optimization_barrier(jnp.sum(exponent, axis=-1, keepdims=True))
    probs_b = probs.astype(jnp.bfloat16)
    attended = batched('hts,hsd->htd', probs_b, values).astype(jnp.bfloat16)
    attended = jnp.swapaxes(attended, 0, 1).reshape(row_count, head_count * head_size)
    grad_heads = jnp.swapaxes(grad_attended.reshape(row_count, head_count, head_size), 0, 1)
    grad_value = batched('hts,htd->hsd', probs_b, grad_heads).astype(jnp.bfloat16)
    grad_probs = batched('htd,hsd->hts', grad_heads, values)
    grad_scores = (probs * (grad_probs - lax.optimization_barrier(jnp.sum(probs * grad_probs, axis=-1, keepdims=True))) * score_scale).astype(jnp.bfloat16)
    grad_qn = batched('hts,hsd->htd', grad_scores, key_b)
    grad_kn = batched('hts,htd->hsd', grad_scores, query_b)
    grad_query = head_norm_back(grad_qn, query_hat, query_inv, q_gain).astype(jnp.bfloat16)
    grad_key = head_norm_back(grad_kn, key_hat, key_inv, k_gain).astype(jnp.bfloat16)
    stacked = jnp.stack([grad_query, grad_key, grad_value], axis=2)
    grad_proj = jnp.transpose(stacked, (1, 0, 2, 3)).reshape(row_count, head_count * 3 * head_size)
    return (attended, grad_proj)

def group_sum(left, right, groups):
    columns = left.shape[1] // groups

    def add_group(group_index, running):
        left_part = lax.dynamic_slice_in_dim(left, group_index * columns, columns, 1)
        right_part = lax.dynamic_slice_in_dim(right, group_index * columns, columns, 1)
        term = lax.dot_general(left_part, right_part, (((1,), (1,)), ((), ())), preferred_element_type=jnp.float32)
        rounded = lax.optimization_barrier(term.astype(jnp.bfloat16))
        return running + rounded.astype(jnp.float32)
    start = jnp.zeros((left.shape[0], right.shape[0]), jnp.float32)
    return lax.fori_loop(0, groups, add_group, start)

def reference(patches, keep_index, keep_count, pack_dest, pack_offset, w_qkv, q_gain, k_gain, w_out, cotangent):
    image_count = keep_count.shape[0]
    slot_lanes = jnp.arange(PATCHES, dtype=jnp.int32)
    target = pack_dest[:, None] * TOK_DEV + pack_offset[:, None] + slot_lanes[None, :]
    live = slot_lanes[None, :] < keep_count[:, None]
    target = jnp.where(live, target, TOKENS).reshape(-1).astype(jnp.int32)
    image_ids = jnp.arange(image_count, dtype=jnp.int32)
    source = (image_ids[:, None] * PATCHES + keep_index).reshape(-1).astype(jnp.int32)
    owners = jnp.broadcast_to(image_ids[:, None], (image_count, PATCHES)).reshape(-1)
    packed = jnp.zeros((TOKENS + 1, D), patches.dtype).at[target].set(patches[source])[:TOKENS]
    segment = jnp.full((TOKENS + 1,), -1, jnp.int32).at[target].set(owners)[:TOKENS]
    valid = segment >= 0
    projected = jnp.dot(packed, w_qkv, preferred_element_type=jnp.float32).astype(jnp.bfloat16)
    grad_rows = jnp.where(valid[:, None], cotangent, jnp.zeros_like(cotangent))
    grad_attended = jnp.dot(grad_rows, w_out, preferred_element_type=jnp.float32).astype(jnp.bfloat16)

    def one_sequence(pieces):
        return attention_pass(pieces[0], pieces[1], q_gain, k_gain, pieces[2])
    attended, grad_proj = lax.map(one_sequence, (projected.reshape(N_DP, TOK_DEV, HEADS, 3, HEAD_DIM), segment.reshape(N_DP, TOK_DEV), grad_attended.reshape(N_DP, TOK_DEV, WIDTH)))
    attended = attended.reshape(TOKENS, WIDTH)
    grad_proj = grad_proj.reshape(TOKENS, 3 * WIDTH)
    proj_sum = group_sum(attended, w_out, N_MP)
    block_out = jnp.where(valid[:, None], packed.astype(jnp.float32) + proj_sum, 0.0).astype(jnp.bfloat16)
    back_sum = group_sum(grad_proj, w_qkv, N_MP)
    grad_packed = (grad_rows.astype(jnp.float32) + back_sum).astype(jnp.bfloat16)
    grad_padded = jnp.concatenate([grad_packed, jnp.zeros((1, D), grad_packed.dtype)], axis=0)
    patch_grad = jnp.zeros((TOKENS, D), grad_packed.dtype).at[source].set(grad_padded[target])
    qkv_grad = jnp.dot(packed.T, grad_proj, preferred_element_type=jnp.float32)
    out_grad = jnp.dot(grad_rows.T, attended, preferred_element_type=jnp.float32)
    return (block_out, patch_grad, qkv_grad, out_grad)
```

```python
import functools

import jax
import jax.numpy as jnp
from jax import lax
from jax.experimental import pallas as pl
from jax.experimental.pallas import tpu as pltpu
from jax.sharding import PartitionSpec as P

MESH = pl.DeviceIdType.MESH
BF, F32 = jnp.bfloat16, jnp.float32
N_DP, RING = 8, 4
ROWS = 384
SLOTS = 48
FEAT = 384
D = 6144
HEAD = 128
HEADS_DEV = 2
QKV = 3 * HEAD * HEADS_DEV
OUT = HEAD * HEADS_DEV
GRAD_ROWS = D // N_DP
HALF, QUART = ROWS // 2, ROWS // 4
EPSILON = 1e-06
SCALE = HEAD ** (-0.5)
N_SEMS = 256


def dot(a, b):
    return jnp.dot(a, b, preferred_element_type=F32)


def dot_nt(a, b):
    return lax.dot_general(a, b, (((1,), (1,)), ((), ())), preferred_element_type=F32)


def dot_tn(a, b):
    return lax.dot_general(a, b, (((0,), (0,)), ((), ())), preferred_element_type=F32)


def head_norm(values):
    centred = values - jnp.mean(values, axis=-1, keepdims=True)
    variance = jnp.mean(centred * centred, axis=-1, keepdims=True)
    inverse = lax.rsqrt(variance + EPSILON)
    return centred * inverse, inverse


def head_norm_back(incoming, normed, inverse, gain):
    scaled = incoming * gain
    return (
        scaled
        - jnp.mean(scaled, axis=-1, keepdims=True)
        - normed * jnp.mean(scaled * normed, axis=-1, keepdims=True)
    ) * inverse


def kernel(
    src_ref, off_ref, qg_ref, kg_ref, patches_ref, cot_ref, wq_hbm, wo_hbm,
    block_ref, pgrad_ref, qkv_ref, out_ref,
    wq, wo, xf, gf, term, pj, gp, att, ga, qb, kb, probs, bias, sel_t, pack, own_x, own_g,
    og, ar, og2, ar2, rb1, rb2, pq, cq, rq, po, co, ro, ssem, rsem, lsem,
):
    dp, mp = lax.axis_index("dp"), lax.axis_index("mp")
    x, c = dp // 2, dp % 2
    y, z = mp // RING, mp % RING
    counter = [0]

    def at_mp(yy, zz):
        return (dp, (yy % RING) * RING + zz % RING)

    def at_dp(xx, cc):
        return ((xx % RING) * 2 + cc, mp)

    def along(axis, step):
        if axis == "y":
            return at_mp(y + RING + step, z)
        if axis == "z":
            return at_mp(y, z + RING + step)
        return at_dp(x + RING + step, c)

    def remote(src, dst, device):
        k = counter[0]
        counter[0] += 1
        return pltpu.make_async_remote_copy(
            src_ref=src, dst_ref=dst, send_sem=ssem.at[k], recv_sem=rsem.at[k],
            device_id=device, device_id_type=MESH,
        )

    sent = {}

    def start(copy):
        copy.start()
        sent[id(copy)] = copy

    def settle(copies):
        for copy in copies:
            sent.pop(id(copy)).wait_send()

    def column(dy, dz):
        block = ((y + dy) % RING) * RING + (z + dz) % RING
        return pl.ds(pl.multiple_of(block * FEAT, 128), FEAT)

    class Gather:
        def __init__(self, full):
            self.full = full
            self.one, self.fwd, self.two, self.fwd2 = {}, {}, {}, {}
            for h in (0, 1):
                a, b = ("y", "z") if h == 0 else ("z", "y")
                for s in (1, -1):
                    self.one[h, s] = self.copy(h, 0, 0, 0, HALF, a, s)
                    self.fwd[h, s] = self.copy(h, -s, 0, 0 if s == 1 else QUART, QUART, a, s)
                    for da in (0, 1, -1, 2):
                        self.two[h, da, s] = self.copy(h, da, 0, 0, HALF, b, s)
                        self.fwd2[h, da, s] = self.copy(h, da, -s, 0 if s == 1 else QUART, QUART, b, s)

        def copy(self, h, da, db, low, n, axis, s):
            dy, dz = (da, db) if h == 0 else (db, da)
            ref = self.full.at[pl.ds(h * HALF + low, n), column(dy + RING, dz + RING)]
            return remote(ref, ref, along(axis, s))

        def begin(self):
            for s in (1, -1):
                for h in (0, 1):
                    start(self.one[h, s])

        def second(self, da):
            for s in (1, -1):
                for h in (0, 1):
                    start(self.two[h, da, s])

        def forward(self, then=True):
            for s in (1, -1):
                for h in (0, 1):
                    self.one[h, s].wait_recv()
                    start(self.fwd[h, s])
            if then:
                self.second(1)
                self.second(-1)

        def opposite(self):
            for s in (1, -1):
                for h in (0, 1):
                    self.fwd[h, s].wait_recv()

        def forward2(self, da):
            for s in (1, -1):
                for h in (0, 1):
                    self.two[h, da, s].wait_recv()
                    start(self.fwd2[h, da, s])

        def copies(self):
            return [copy for group in (self.one, self.fwd, self.two, self.fwd2) for copy in group.values()]

        def finish(self, das=(0, 1, -1, 2)):
            for da in das:
                for s in (1, -1):
                    for h in (0, 1):
                        self.fwd2[h, da, s].wait_recv()

    class Ring:
        def __init__(self, part, box, rows, axis, chunk=None):
            half = rows // 2
            self.part, self.box, self.rows, self.half = part, box, rows, half
            self.chunk = chunk
            self.c0 = remote(part(2, 0, half), box(0, half), along(axis, 1))
            self.c1 = remote(part(2, half, half), box(half, half), along(axis, -1))
            self.c2 = remote(part(1, half, half), box(rows + half, half), along(axis, 1))
            self.c3 = remote(part(3, 0, half), box(2 * rows, half), along(axis, -1))
            self.c4 = remote(part(1, 0, half), box(rows, half), along(axis, 1))
            self.c5 = remote(part(3, half, half), box(2 * rows + half, half), along(axis, -1))

        def far(self):
            start(self.c0)
            start(self.c1)

        def near(self):
            start(self.c2)
            start(self.c3)

        def add(self, r, low, box_low):
            if self.chunk is None:
                ref = self.part(r, low, self.half)
                ref[...] = (ref[...].astype(F32) + self.box(box_low, self.half)[...].astype(F32)).astype(BF)
                return

            @pl.loop(0, self.half // self.chunk)
            def _(i):
                step = pl.multiple_of(i * self.chunk, self.chunk)
                ref = self.part(r, low + step, self.chunk)
                ref[...] = (ref[...].astype(F32) + self.box(box_low + step, self.chunk)[...].astype(F32)).astype(BF)

        def pass_on(self):
            self.c0.wait_recv()
            self.add(1, 0, 0)
            start(self.c4)
            self.c1.wait_recv()
            self.add(3, self.half, self.half)
            start(self.c5)

        def arrive(self):
            for copy in (self.c2, self.c3, self.c4, self.c5):
                copy.wait_recv()

        def total(self, low, n):
            return (
                self.part(0, low, n)[...].astype(F32)
                + self.box(self.rows + low, n)[...].astype(F32)
                + self.box(2 * self.rows + low, n)[...].astype(F32)
            )

    class Scatter:
        def __init__(self, terms, boxes):
            self.first, self.last = {}, {}
            for h in (0, 1):
                a, b = ("z", "y") if h == 0 else ("y", "z")

                def piece(r1, r2, low, n, h=h):
                    slot = r2 * RING + r1 if h == 0 else r1 * RING + r2
                    return terms.at[pl.ds(h * HALF + low, n), pl.ds(slot * FEAT, FEAT)]

                for r2 in range(RING):
                    self.first[h, r2] = Ring(
                        lambda r, low, n, r2=r2, piece=piece: piece(r, r2, low, n),
                        lambda low, n, h=h, r2=r2: boxes.at[h, r2, pl.ds(low, n)],
                        HALF, a,
                    )
                self.last[h] = Ring(
                    lambda r, low, n, piece=piece: piece(0, r, low, n),
                    lambda low, n, h=h: boxes.at[h, RING, pl.ds(low, n)],
                    HALF, b,
                )

        def send(self, r2):
            for h in (0, 1):
                self.first[h, r2].far()
            for h in (0, 1):
                self.first[h, r2].near()

        def pass_on(self, r2):
            for h in (0, 1):
                self.first[h, r2].pass_on()

        def collect(self, r2):
            for h in (0, 1):
                ring = self.first[h, r2]
                ring.arrive()
                ring.part(0, 0, HALF)[...] = ring.total(0, HALF).astype(BF)
                if r2 == 2:
                    self.last[h].far()
            if r2 == 3:
                for h in (0, 1):
                    self.last[h].near()

        def last_pass(self):
            for h in (0, 1):
                self.last[h].pass_on()

        def result(self, h):
            self.last[h].arrive()
            return self.last[h].total(0, HALF)

    class WeightGrad:
        def __init__(self, rows, cols, width, mine, theirs, boxes, slots, result):
            self.rows, self.cols, self.mine, self.theirs, self.result = rows, cols, mine, theirs, result
            self.slots = slots
            self.swap = {
                dx: remote(mine.at[i % slots], theirs.at[dx], at_dp(x, 1 - c)) for i, dx in enumerate((2, 1, 3, 0))
            }
            self.ring = Ring(
                lambda r, low, n: theirs.at[r, pl.ds(low, n)], lambda low, n: boxes.at[pl.ds(low, n)],
                GRAD_ROWS, "x", chunk=64,
            )
            self.order = []

        def tile(self, dx, core, m):
            block = ((x + dx) % RING) * 2 + core
            left = self.rows[:, pl.ds(pl.multiple_of(block * GRAD_ROWS + m * 256, 128), 256)]
            return dot_tn(left, self.cols[...])

        def send(self, dx):
            i = len(self.order)
            if i >= self.slots:
                self.swap[self.order[i - self.slots]].wait_send()
            self.order.append(dx)
            slot = i % self.slots

            @pl.loop(0, GRAD_ROWS // 256)
            def _(m):
                self.mine[slot, pl.ds(pl.multiple_of(m * 256, 256), 256), :] = self.tile(dx, 1 - c, m).astype(BF)

            self.swap[dx].start()

        def add(self, dx):
            self.swap[dx].wait_recv()

            @pl.loop(0, GRAD_ROWS // 256)
            def _(m):
                at = pl.ds(pl.multiple_of(m * 256, 256), 256)
                value = self.tile(dx, c, m) + self.theirs[dx, at, :].astype(F32)
                if dx == 0:
                    self.result[at, :] = value
                else:
                    self.theirs[dx, at, :] = value.astype(BF)

            if dx == 2:
                self.ring.far()
            if dx == 3:
                self.ring.near()

        def finish(self):
            self.ring.arrive()

            @pl.loop(0, GRAD_ROWS // 64)
            def _(i):
                low = pl.multiple_of(i * 64, 64)
                at = pl.ds(low, 64)
                self.result[at, :] = (
                    self.result[at, :]
                    + self.ring.box(GRAD_ROWS + low, 64)[...].astype(F32)
                    + self.ring.box(2 * GRAD_ROWS + low, 64)[...].astype(F32)
                )

        def close(self):
            for dx in self.order[-self.slots:]:
                self.swap[dx].wait_send()

    load_q = pltpu.make_async_copy(wq_hbm, wq, lsem.at[0])
    load_o = pltpu.make_async_copy(wo_hbm, wo, lsem.at[1])
    load_q.start()
    load_o.start()

    barrier = pltpu.get_barrier_semaphore()
    for axis in ("y", "z"):
        for s in (1, -1):
            pl.semaphore_signal(barrier, inc=1, device_id=along(axis, s), device_id_type=MESH)
    for o in range(1, N_DP):
        pl.semaphore_signal(barrier, inc=1, device_id=((dp + o) % N_DP, mp), device_id_type=MESH)

    off = off_ref[...]
    total_rows = jnp.sum((off >= 0).astype(F32), axis=1, keepdims=True)
    row_id = lax.broadcasted_iota(jnp.int32, (ROWS, ROWS), 0)
    col_id = lax.broadcasted_iota(jnp.int32, (ROWS, ROWS), 1)
    row_live = row_id.astype(F32) < total_rows
    col_live = col_id.astype(F32) < total_rows
    sel_t[...] = (row_id == src_ref[...]).astype(F32).astype(BF)
    pack[...] = (row_id == off).astype(F32).astype(BF)
    own_g[...] = jnp.where(row_live, cot_ref[...].astype(F32), 0.0).astype(BF)
    gf[:, column(0, 0)] = own_g[...]
    og[...] = dot_tn(sel_t[...], patches_ref[...]).astype(BF)

    gather_g, gather_x = Gather(gf), Gather(xf)
    swap_x = [
        remote(og.at[pl.ds(pl.multiple_of(((dp + o) % N_DP) * SLOTS, SLOTS), SLOTS)],
               ar.at[pl.ds(pl.multiple_of(dp * SLOTS, SLOTS), SLOTS)], ((dp + o) % N_DP, mp))
        for o in range(1, N_DP)
    ]
    swap_g = [
        remote(og2.at[pl.ds(pl.multiple_of(((dp + o) % N_DP) * SLOTS, SLOTS), SLOTS)],
               ar2.at[pl.ds(pl.multiple_of(dp * SLOTS, SLOTS), SLOTS)], ((dp + o) % N_DP, mp))
        for o in range(1, N_DP)
    ]
    scatter_p, scatter_b = Scatter(term, rb1), Scatter(gf, rb2)
    grad_q = WeightGrad(xf, gp, QKV, pq, cq, rq, 2, qkv_ref)
    grad_o = WeightGrad(gf, att, OUT, po, co, ro, 4, out_ref)
    assert counter[0] <= N_SEMS

    pl.semaphore_wait(barrier, 4 + N_DP - 1)
    for copy in swap_x:
        start(copy)
    gather_g.begin()
    here = pl.ds(pl.multiple_of(dp * SLOTS, SLOTS), SLOTS)
    ar[here, :] = og[here, :]
    same = ((row_id * 1366) >> 16) == ((col_id * 1366) >> 16)
    image = dot(pack[...], same.astype(F32).astype(BF)).astype(BF)
    both = dot_nt(image, pack[...]) > 0.5
    bias[...] = jnp.where(both | (jnp.logical_not(row_live) & jnp.logical_not(col_live)), 0.0, -jnp.inf)
    for copy in swap_x:
        copy.wait_recv()
    own_x[...] = dot(pack[...], ar[...]).astype(BF)
    xf[:, column(0, 0)] = own_x[...]
    gather_x.begin()
    gather_x.second(0)
    gather_g.forward(then=False)
    gather_x.forward()
    gather_g.opposite()
    gather_x.opposite()
    gather_x.second(2)
    for da in (0, 1, -1):
        gather_x.forward2(da)
    for da in (0, 1, -1, 2):
        gather_g.second(da)
    gather_x.forward2(2)
    gather_x.finish()
    load_q.wait()
    load_o.wait()

    def project(low, high):
        @pl.loop(low, high)
        def _(k):
            at = pl.ds(pl.multiple_of(k * 768, 768), 768)
            part = dot(xf[:, at], wq[at, :])

            @pl.when(k == 0)
            def _():
                qkv_ref[0:ROWS, :] = part

            @pl.when(k > 0)
            def _():
                qkv_ref[0:ROWS, :] += part

    def head_forward(h):
        base = h * 3 * HEAD
        query, _ = head_norm(pj[:, base:base + HEAD].astype(F32))
        keys, _ = head_norm(pj[:, base + HEAD:base + 2 * HEAD].astype(F32))
        qb[h] = (query * qg_ref[...]).astype(BF)
        kb[h] = (keys * kg_ref[...]).astype(BF)
        scores = dot_nt(qb[h], kb[h]) * SCALE + bias[...]
        exponent = jnp.exp(scores - jnp.max(scores, axis=-1, keepdims=True))
        prob = exponent / jnp.sum(exponent, axis=-1, keepdims=True)
        probs[h] = prob
        att[:, h * HEAD:(h + 1) * HEAD] = dot(prob.astype(BF), pj[:, base + 2 * HEAD:base + 3 * HEAD]).astype(BF)

    def head_backward(h):
        base = h * 3 * HEAD
        value = pj[:, base + 2 * HEAD:base + 3 * HEAD]
        incoming = ga[:, h * HEAD:(h + 1) * HEAD]
        prob = probs[h]
        gp[:, base + 2 * HEAD:base + 3 * HEAD] = dot_tn(prob.astype(BF), incoming).astype(BF)
        grad_probs = dot_nt(incoming, value)
        grad_scores = (prob * (grad_probs - jnp.sum(prob * grad_probs, axis=-1, keepdims=True)) * SCALE).astype(BF)
        query, query_inv = head_norm(pj[:, base:base + HEAD].astype(F32))
        keys, key_inv = head_norm(pj[:, base + HEAD:base + 2 * HEAD].astype(F32))
        grad_qn = dot(grad_scores, kb[h])
        grad_kn = dot_tn(grad_scores, qb[h])
        gp[:, base:base + HEAD] = head_norm_back(grad_qn, query, query_inv, qg_ref[...]).astype(BF)
        gp[:, base + HEAD:base + 2 * HEAD] = head_norm_back(grad_kn, keys, key_inv, kg_ref[...]).astype(BF)

    def make_terms(low, high, left, weights, terms):
        @pl.loop(low, high)
        def _(j):
            block = ((y + j // RING) % RING) * RING + (z + j % RING) % RING
            at = pl.ds(pl.multiple_of(block * FEAT, 128), FEAT)
            value = dot_nt(left[...], weights[at, :]).astype(BF)
            terms[:, pl.ds(pl.multiple_of(j * FEAT, 128), FEAT)] = value

    project(0, 3)
    gather_g.forward2(0)
    project(3, 6)
    gather_g.forward2(1)
    project(6, 8)
    pj[...] = qkv_ref[0:ROWS, :].astype(BF)
    gather_g.forward2(-1)
    head_forward(0)
    gather_g.forward2(2)
    head_forward(1)
    make_terms(0, 16, att, wo, term)
    for r2 in (2, 1, 3, 0):
        scatter_p.send(r2)
    gather_g.finish()

    def grad_attended():
        @pl.loop(0, 8)
        def _(k):
            at = pl.ds(pl.multiple_of(k * 768, 768), 768)
            part = dot(gf[:, at], wo[at, :])

            @pl.when(k == 0)
            def _():
                qkv_ref[0:ROWS, 0:OUT] = part

            @pl.when(k > 0)
            def _():
                qkv_ref[0:ROWS, 0:OUT] += part

        ga[...] = qkv_ref[0:ROWS, 0:OUT].astype(BF)

    grad_o.send(2)
    grad_o.send(1)
    grad_o.add(2)
    grad_attended()
    scatter_p.pass_on(2)
    head_backward(0)
    scatter_p.pass_on(1)
    head_backward(1)
    scatter_p.pass_on(3)
    grad_q.send(2)
    grad_o.send(3)
    grad_o.send(0)
    grad_o.add(1)
    grad_o.add(3)
    grad_q.add(2)
    scatter_p.pass_on(0)
    scatter_p.collect(2)
    grad_q.send(1)
    grad_q.add(1)
    grad_o.add(0)
    scatter_p.collect(1)
    scatter_p.collect(3)
    grad_q.send(3)
    grad_q.add(3)
    grad_o.ring.pass_on()
    settle(gather_g.copies())
    make_terms(0, 16, gp, wq, gf)
    scatter_p.last_pass()
    for r2 in (2, 1, 3, 0):
        scatter_b.send(r2)
    scatter_p.collect(0)
    grad_q.send(0)
    grad_q.add(0)
    for h in (0, 1):
        rows = pl.ds(h * HALF, HALF)
        live = lax.broadcasted_iota(jnp.int32, (HALF, FEAT), 0).astype(F32) + float(h * HALF) < total_rows
        value = own_x[rows, :].astype(F32) + scatter_p.result(h)
        block_ref[rows, :] = jnp.where(live, value, 0.0).astype(BF)
    scatter_b.pass_on(2)
    scatter_b.pass_on(1)
    scatter_b.pass_on(3)
    scatter_b.pass_on(0)
    grad_o.finish()
    scatter_b.collect(2)
    grad_q.ring.pass_on()
    scatter_b.collect(1)
    scatter_b.collect(3)
    scatter_b.last_pass()
    scatter_b.collect(0)
    for h in (0, 1):
        rows = pl.ds(h * HALF, HALF)
        own_g[rows, :] = (own_g[rows, :].astype(F32) + scatter_b.result(h)).astype(BF)
    og2[...] = dot_tn(pack[...], own_g[...]).astype(BF)
    for copy in swap_g:
        start(copy)
    ar2[here, :] = og2[here, :]
    grad_q.finish()
    for copy in swap_g:
        copy.wait_recv()
    pgrad_ref[...] = dot(sel_t[...], ar2[...]).astype(BF)
    grad_q.close()
    grad_o.close()
    settle(list(sent.values()))


def shards(
    patches, keep_index, keep_count, pack_dest, pack_offset, w_qkv, q_gain, k_gain, w_out, cotangent
):
    shard = lax.axis_index("dp")
    places = jnp.arange(N_DP, dtype=jnp.int32)
    lanes = jnp.arange(SLOTS, dtype=jnp.int32)
    dest = pack_dest.reshape(N_DP, N_DP)
    count = keep_count.reshape(N_DP, N_DP)
    offset = pack_offset.reshape(N_DP, N_DP)
    my_dest = lax.dynamic_index_in_dim(dest, shard, 0, keepdims=False)
    my_count = lax.dynamic_index_in_dim(count, shard, 0, keepdims=False)
    rows = keep_index + places[:, None] * SLOTS + 1
    rows = jnp.where(lanes[None, :] < my_count[:, None], rows, 0)
    source = jnp.sum(jnp.where(my_dest[None, :, None] == places[:, None, None], rows[None], 0), axis=1) - 1
    mine = dest == shard
    got = jnp.sum(jnp.where(mine, count, 0), axis=1)
    base = jnp.sum(jnp.where(mine, offset, 0), axis=1)
    target = jnp.where(lanes[None, :] < got[:, None], base[:, None] + lanes[None, :], -1)

    vmem = pl.BlockSpec(memory_space=pltpu.VMEM)
    hbm = pl.BlockSpec(memory_space=pltpu.HBM)
    return pl.pallas_call(
        kernel,
        out_shape=(
            jax.ShapeDtypeStruct((ROWS, FEAT), BF),
            jax.ShapeDtypeStruct((ROWS, FEAT), BF),
            jax.ShapeDtypeStruct((GRAD_ROWS, QKV), F32),
            jax.ShapeDtypeStruct((GRAD_ROWS, OUT), F32),
        ),
        in_specs=[vmem] * 6 + [hbm] * 2,
        out_specs=(vmem,) * 4,
        scratch_shapes=[
            pltpu.VMEM((D, QKV), BF),
            pltpu.VMEM((D, OUT), BF),
            pltpu.VMEM((ROWS, D), BF),
            pltpu.VMEM((ROWS, D), BF),
            pltpu.VMEM((ROWS, D), BF),
            pltpu.VMEM((ROWS, QKV), BF),
            pltpu.VMEM((ROWS, QKV), BF),
            pltpu.VMEM((ROWS, OUT), BF),
            pltpu.VMEM((ROWS, OUT), BF),
            pltpu.VMEM((HEADS_DEV, ROWS, HEAD), BF),
            pltpu.VMEM((HEADS_DEV, ROWS, HEAD), BF),
            pltpu.VMEM((HEADS_DEV, ROWS, ROWS), F32),
            pltpu.VMEM((ROWS, ROWS), F32),
            pltpu.VMEM((ROWS, ROWS), BF),
            pltpu.VMEM((ROWS, ROWS), BF),
            pltpu.VMEM((ROWS, FEAT), BF),
            pltpu.VMEM((ROWS, FEAT), BF),
            pltpu.VMEM((ROWS, FEAT), BF),
            pltpu.VMEM((ROWS, FEAT), BF),
            pltpu.VMEM((ROWS, FEAT), BF),
            pltpu.VMEM((ROWS, FEAT), BF),
            pltpu.VMEM((2, RING + 1, 3 * HALF, FEAT), BF),
            pltpu.VMEM((2, RING + 1, 3 * HALF, FEAT), BF),
            pltpu.VMEM((2, GRAD_ROWS, QKV), BF),
            pltpu.VMEM((RING, GRAD_ROWS, QKV), BF),
            pltpu.VMEM((3 * GRAD_ROWS, QKV), BF),
            pltpu.VMEM((4, GRAD_ROWS, OUT), BF),
            pltpu.VMEM((RING, GRAD_ROWS, OUT), BF),
            pltpu.VMEM((3 * GRAD_ROWS, OUT), BF),
            pltpu.SemaphoreType.DMA((N_SEMS,)),
            pltpu.SemaphoreType.DMA((N_SEMS,)),
            pltpu.SemaphoreType.DMA((2,)),
        ],
        compiler_params=pltpu.CompilerParams(
            collective_id=0, has_side_effects=True, vmem_limit_bytes=63 << 20
        ),
        cost_estimate=pl.CostEstimate(flops=15_000_000_000, bytes_accessed=20_000_000, transcendentals=300_000),
        name="block",
    )(
        source.reshape(1, ROWS), target.reshape(1, ROWS), q_gain.reshape(1, HEAD), k_gain.reshape(1, HEAD),
        patches, cotangent, w_qkv, w_out,
    )


def solution(mesh):
    placed = (
        P("dp", "mp"), P("dp", None), P(), P(), P(), P(None, "mp"), P(), P(), P(None, "mp"), P("dp", "mp"),
    )
    return jax.shard_map(
        shards, mesh=mesh, in_specs=placed, out_specs=(P("dp", "mp"),) * 4, check_vma=False,
    )
```

```python
import functools

import jax
import jax.numpy as jnp
from jax import lax
from jax.experimental import pallas as pl
from jax.experimental.pallas import tpu as pltpu
from jax.sharding import PartitionSpec as P

MESH = pl.DeviceIdType.MESH
BF, F32 = jnp.bfloat16, jnp.float32
N_DP, RING = 8, 4
ROWS = 384
SLOTS = 48
FEAT = 384
D = 6144
HEAD = 128
HEADS_DEV = 2
QKV = 3 * HEAD * HEADS_DEV
OUT = HEAD * HEADS_DEV
GRAD_ROWS = D // N_DP
HALF, QUART = ROWS // 2, ROWS // 4
EPSILON = 1e-06
SCALE = HEAD ** (-0.5)
N_SEMS = 256


def dot(a, b):
    return jnp.dot(a, b, preferred_element_type=F32)


def dot_nt(a, b):
    return lax.dot_general(a, b, (((1,), (1,)), ((), ())), preferred_element_type=F32)


def dot_tn(a, b):
    return lax.dot_general(a, b, (((0,), (0,)), ((), ())), preferred_element_type=F32)


def head_norm(values):
    centred = values - jnp.mean(values, axis=-1, keepdims=True)
    variance = jnp.mean(centred * centred, axis=-1, keepdims=True)
    inverse = lax.rsqrt(variance + EPSILON)
    return centred * inverse, inverse


def head_norm_back(incoming, normed, inverse, gain):
    scaled = incoming * gain
    return (
        scaled
        - jnp.mean(scaled, axis=-1, keepdims=True)
        - normed * jnp.mean(scaled * normed, axis=-1, keepdims=True)
    ) * inverse


def kernel(
    count_ref, dest_ref, offset_ref, keep_ref, qg_ref, kg_ref, patches_ref, cot_ref, wq_hbm, wo_hbm,
    block_hbm, pgrad_hbm, qkv_hbm, out_hbm,
    block_ref, pgrad_ref, qkv_ref, out_ref,
    wq, wo, xf, gf, term, pj, gp, att, ga, qb, kb, probs, bias, sel_t, pack, own_x, own_g,
    og, ar, og2, ar2, rb1, rb2, pq, cq, rq, po, co, ro, ssem, rsem, lsem,
):
    dp, mp = lax.axis_index("dp"), lax.axis_index("mp")
    x, c = dp // 2, dp % 2
    y, z = mp // RING, mp % RING
    counter = [0]

    def at_mp(yy, zz):
        return (dp, (yy % RING) * RING + zz % RING)

    def at_dp(xx, cc):
        return ((xx % RING) * 2 + cc, mp)

    def along(axis, step):
        if axis == "y":
            return at_mp(y + RING + step, z)
        if axis == "z":
            return at_mp(y, z + RING + step)
        return at_dp(x + RING + step, c)

    def remote(src, dst, device):
        k = counter[0]
        counter[0] += 1
        return pltpu.make_async_remote_copy(
            src_ref=src, dst_ref=dst, send_sem=ssem.at[k], recv_sem=rsem.at[k],
            device_id=device, device_id_type=MESH,
        )

    sent = {}

    def start(copy):
        copy.start()
        sent[id(copy)] = copy

    def settle(copies):
        for copy in copies:
            sent.pop(id(copy)).wait_send()

    def column(dy, dz):
        block = ((y + dy) % RING) * RING + (z + dz) % RING
        return pl.ds(pl.multiple_of(block * FEAT, 128), FEAT)

    class Gather:
        def __init__(self, full):
            self.full = full
            self.one, self.fwd, self.two, self.fwd2 = {}, {}, {}, {}
            for h in (0, 1):
                a, b = ("y", "z") if h == 0 else ("z", "y")
                for s in (1, -1):
                    self.one[h, s] = self.copy(h, 0, 0, 0, HALF, a, s)
                    self.fwd[h, s] = self.copy(h, -s, 0, 0 if s == 1 else QUART, QUART, a, s)
                    for da in (0, 1, -1, 2):
                        self.two[h, da, s] = self.copy(h, da, 0, 0, HALF, b, s)
                        self.fwd2[h, da, s] = self.copy(h, da, -s, 0 if s == 1 else QUART, QUART, b, s)

        def copy(self, h, da, db, low, n, axis, s):
            dy, dz = (da, db) if h == 0 else (db, da)
            ref = self.full.at[pl.ds(h * HALF + low, n), column(dy + RING, dz + RING)]
            return remote(ref, ref, along(axis, s))

        def begin(self):
            for s in (1, -1):
                for h in (0, 1):
                    start(self.one[h, s])

        def second(self, da):
            for s in (1, -1):
                for h in (0, 1):
                    start(self.two[h, da, s])

        def forward(self, then=True):
            for s in (1, -1):
                for h in (0, 1):
                    self.one[h, s].wait_recv()
                    start(self.fwd[h, s])
            if then:
                self.second(1)
                self.second(-1)

        def opposite(self):
            for s in (1, -1):
                for h in (0, 1):
                    self.fwd[h, s].wait_recv()

        def forward2(self, da):
            for s in (1, -1):
                for h in (0, 1):
                    self.two[h, da, s].wait_recv()
                    start(self.fwd2[h, da, s])

        def copies(self):
            return [copy for group in (self.one, self.fwd, self.two, self.fwd2) for copy in group.values()]

        def finish(self, das=(0, 1, -1, 2)):
            for da in das:
                for s in (1, -1):
                    for h in (0, 1):
                        self.fwd2[h, da, s].wait_recv()

    class Ring:
        def __init__(self, part, box, rows, axis, chunk=None):
            half = rows // 2
            self.part, self.box, self.rows, self.half = part, box, rows, half
            self.chunk = chunk
            self.c0 = remote(part(2, 0, half), box(0, half), along(axis, 1))
            self.c1 = remote(part(2, half, half), box(half, half), along(axis, -1))
            self.c2 = remote(part(1, half, half), box(rows + half, half), along(axis, 1))
            self.c3 = remote(part(3, 0, half), box(2 * rows, half), along(axis, -1))
            self.c4 = remote(part(1, 0, half), box(rows, half), along(axis, 1))
            self.c5 = remote(part(3, half, half), box(2 * rows + half, half), along(axis, -1))

        def far(self):
            start(self.c0)
            start(self.c1)

        def near(self):
            start(self.c2)
            start(self.c3)

        def add(self, r, low, box_low):
            if self.chunk is None:
                ref = self.part(r, low, self.half)
                ref[...] = (ref[...].astype(F32) + self.box(box_low, self.half)[...].astype(F32)).astype(BF)
                return

            @pl.loop(0, self.half // self.chunk)
            def _(i):
                step = pl.multiple_of(i * self.chunk, self.chunk)
                ref = self.part(r, low + step, self.chunk)
                ref[...] = (ref[...].astype(F32) + self.box(box_low + step, self.chunk)[...].astype(F32)).astype(BF)

        def pass_on(self):
            self.c0.wait_recv()
            self.add(1, 0, 0)
            start(self.c4)
            self.c1.wait_recv()
            self.add(3, self.half, self.half)
            start(self.c5)

        def arrive(self):
            for copy in (self.c2, self.c3, self.c4, self.c5):
                copy.wait_recv()

        def total(self, low, n):
            return (
                self.part(0, low, n)[...].astype(F32)
                + self.box(self.rows + low, n)[...].astype(F32)
                + self.box(2 * self.rows + low, n)[...].astype(F32)
            )

    class Scatter:
        def __init__(self, terms, boxes):
            self.first, self.last = {}, {}
            for h in (0, 1):
                a, b = ("z", "y") if h == 0 else ("y", "z")

                def piece(r1, r2, low, n, h=h):
                    slot = r2 * RING + r1 if h == 0 else r1 * RING + r2
                    return terms.at[pl.ds(h * HALF + low, n), pl.ds(slot * FEAT, FEAT)]

                for r2 in range(RING):
                    self.first[h, r2] = Ring(
                        lambda r, low, n, r2=r2, piece=piece: piece(r, r2, low, n),
                        lambda low, n, h=h, r2=r2: boxes.at[h, r2, pl.ds(low, n)],
                        HALF, a,
                    )
                self.last[h] = Ring(
                    lambda r, low, n, piece=piece: piece(0, r, low, n),
                    lambda low, n, h=h: boxes.at[h, RING, pl.ds(low, n)],
                    HALF, b,
                )

        def send(self, r2):
            for h in (0, 1):
                self.first[h, r2].far()
            for h in (0, 1):
                self.first[h, r2].near()

        def pass_on(self, r2):
            for h in (0, 1):
                self.first[h, r2].pass_on()

        def collect(self, r2):
            for h in (0, 1):
                ring = self.first[h, r2]
                ring.arrive()
                ring.part(0, 0, HALF)[...] = ring.total(0, HALF).astype(BF)
                if r2 == 2:
                    self.last[h].far()
            if r2 == 3:
                for h in (0, 1):
                    self.last[h].near()

        def last_pass(self):
            for h in (0, 1):
                self.last[h].pass_on()

        def result(self, h):
            self.last[h].arrive()
            return self.last[h].total(0, HALF)

    class WeightGrad:
        def __init__(self, rows, cols, width, mine, theirs, boxes, slots, result):
            self.rows, self.cols, self.mine, self.theirs, self.result = rows, cols, mine, theirs, result
            self.slots = slots
            self.swap = {
                dx: remote(mine.at[i % slots], theirs.at[dx], at_dp(x, 1 - c)) for i, dx in enumerate((2, 1, 3, 0))
            }
            self.ring = Ring(
                lambda r, low, n: theirs.at[r, pl.ds(low, n)], lambda low, n: boxes.at[pl.ds(low, n)],
                GRAD_ROWS, "x", chunk=64,
            )
            self.order = []

        def tile(self, dx, core, m):
            block = ((x + dx) % RING) * 2 + core
            left = self.rows[:, pl.ds(pl.multiple_of(block * GRAD_ROWS + m * 256, 128), 256)]
            return dot_tn(left, self.cols[...])

        def send(self, dx):
            i = len(self.order)
            if i >= self.slots:
                self.swap[self.order[i - self.slots]].wait_send()
            self.order.append(dx)
            slot = i % self.slots

            @pl.loop(0, GRAD_ROWS // 256)
            def _(m):
                self.mine[slot, pl.ds(pl.multiple_of(m * 256, 256), 256), :] = self.tile(dx, 1 - c, m).astype(BF)

            self.swap[dx].start()

        def add(self, dx):
            self.swap[dx].wait_recv()

            @pl.loop(0, GRAD_ROWS // 256)
            def _(m):
                at = pl.ds(pl.multiple_of(m * 256, 256), 256)
                value = self.tile(dx, c, m) + self.theirs[dx, at, :].astype(F32)
                if dx == 0:
                    self.result[at, :] = value
                else:
                    self.theirs[dx, at, :] = value.astype(BF)

            if dx == 2:
                self.ring.far()
            if dx == 3:
                self.ring.near()

        def finish(self):
            self.ring.arrive()

            @pl.loop(0, GRAD_ROWS // 64)
            def _(i):
                low = pl.multiple_of(i * 64, 64)
                at = pl.ds(low, 64)
                self.result[at, :] = (
                    self.result[at, :]
                    + self.ring.box(GRAD_ROWS + low, 64)[...].astype(F32)
                    + self.ring.box(2 * GRAD_ROWS + low, 64)[...].astype(F32)
                )

        def close(self):
            for dx in self.order[-self.slots:]:
                self.swap[dx].wait_send()

    load_q = pltpu.make_async_copy(wq_hbm, wq, lsem.at[0])
    load_o = pltpu.make_async_copy(wo_hbm, wo, lsem.at[1])
    load_q.start()
    load_o.start()

    barrier = pltpu.get_barrier_semaphore()
    for axis in ("y", "z"):
        for s in (1, -1):
            pl.semaphore_signal(barrier, inc=1, device_id=along(axis, s), device_id_type=MESH)
    for o in range(1, N_DP):
        pl.semaphore_signal(barrier, inc=1, device_id=((dp + o) % N_DP, mp), device_id_type=MESH)

    def saved(copy):
        copy.start()
        saves.append(copy)

    saves = []
    lane = lax.broadcasted_iota(jnp.int32, (1, ROWS), 1)
    part = (lane * 1366) >> 16
    slot = lane - part * SLOTS
    off = jnp.full((1, ROWS), -1, jnp.int32)
    total_rows = 0
    for t in range(N_DP):
        base, here_count = 0, 0
        for k in range(N_DP):
            mine = dest_ref[t * N_DP + k] == dp
            base += jnp.where(mine, offset_ref[t * N_DP + k], 0)
            here_count += jnp.where(mine, count_ref[t * N_DP + k], 0)
        off = jnp.where((part == t) & (slot < here_count), base + slot, off)
        total_rows += here_count
    spread_row = lax.broadcasted_iota(jnp.int32, (SLOTS, ROWS), 0)
    spread = (spread_row == slot).astype(F32).astype(BF)
    kept = dot(keep_ref[...].astype(F32).astype(BF), spread).astype(jnp.int32)
    src = jnp.full((1, ROWS), -1, jnp.int32)
    for k in range(N_DP):
        goes = (part == dest_ref[dp * N_DP + k]) & (slot < count_ref[dp * N_DP + k])
        src = jnp.where(goes, kept[k:k + 1, :] + k * SLOTS, src)
    row_id = lax.broadcasted_iota(jnp.int32, (ROWS, ROWS), 0)
    col_id = lax.broadcasted_iota(jnp.int32, (ROWS, ROWS), 1)
    row_live = row_id < total_rows
    col_live = col_id < total_rows
    own_g[...] = jnp.where(row_live, cot_ref[...].astype(F32), 0.0).astype(BF)
    gf[:, column(0, 0)] = own_g[...]
    sel_t[...] = (row_id == src).astype(F32).astype(BF)
    og[...] = dot_tn(sel_t[...], patches_ref[...]).astype(BF)

    gather_g, gather_x = Gather(gf), Gather(xf)
    swap_x = [
        remote(og.at[pl.ds(pl.multiple_of(((dp + o) % N_DP) * SLOTS, SLOTS), SLOTS)],
               ar.at[pl.ds(pl.multiple_of(dp * SLOTS, SLOTS), SLOTS)], ((dp + o) % N_DP, mp))
        for o in range(1, N_DP)
    ]
    swap_g = [
        remote(og2.at[pl.ds(pl.multiple_of(((dp + o) % N_DP) * SLOTS, SLOTS), SLOTS)],
               ar2.at[pl.ds(pl.multiple_of(dp * SLOTS, SLOTS), SLOTS)], ((dp + o) % N_DP, mp))
        for o in range(1, N_DP)
    ]
    scatter_p, scatter_b = Scatter(term, rb1), Scatter(gf, rb2)
    grad_q = WeightGrad(xf, gp, QKV, pq, cq, rq, 2, qkv_ref)
    grad_o = WeightGrad(gf, att, OUT, po, co, ro, 4, out_ref)
    assert counter[0] <= N_SEMS

    pl.semaphore_wait(barrier, 4 + N_DP - 1)
    for copy in swap_x:
        start(copy)
    gather_g.begin()
    here = pl.ds(pl.multiple_of(dp * SLOTS, SLOTS), SLOTS)
    ar[here, :] = og[here, :]
    pack[...] = (row_id == off).astype(F32).astype(BF)
    for copy in swap_x:
        copy.wait_recv()
    own_x[...] = dot(pack[...], ar[...]).astype(BF)
    xf[:, column(0, 0)] = own_x[...]
    gather_x.begin()
    gather_x.second(0)
    gather_g.forward(then=False)
    gather_x.forward()
    gather_g.opposite()
    gather_x.opposite()
    gather_x.second(2)
    same = ((row_id * 1366) >> 16) == ((col_id * 1366) >> 16)
    image = dot(pack[...], same.astype(F32).astype(BF)).astype(BF)
    both = dot_nt(image, pack[...]) > 0.5
    bias[...] = jnp.where(both | (jnp.logical_not(row_live) & jnp.logical_not(col_live)), 0.0, -jnp.inf)
    for da in (0, 1, -1):
        gather_x.forward2(da)
    gather_g.second(0)
    gather_x.forward2(2)
    for da in (1, -1, 2):
        gather_g.second(da)
    gather_x.finish()
    load_q.wait()

    def project(low, high):
        @pl.loop(low, high)
        def _(k):
            at = pl.ds(pl.multiple_of(k * 768, 768), 768)
            part = dot(xf[:, at], wq[at, :])

            @pl.when(k == 0)
            def _():
                qkv_ref[0:ROWS, :] = part

            @pl.when(k > 0)
            def _():
                qkv_ref[0:ROWS, :] += part

    def head_forward(h):
        base = h * 3 * HEAD
        query, _ = head_norm(pj[:, base:base + HEAD].astype(F32))
        keys, _ = head_norm(pj[:, base + HEAD:base + 2 * HEAD].astype(F32))
        qb[h] = (query * qg_ref[...]).astype(BF)
        kb[h] = (keys * kg_ref[...]).astype(BF)
        scores = dot_nt(qb[h], kb[h]) * SCALE + bias[...]
        exponent = jnp.exp(scores - jnp.max(scores, axis=-1, keepdims=True))
        prob = exponent / jnp.sum(exponent, axis=-1, keepdims=True)
        probs[h] = prob
        att[:, h * HEAD:(h + 1) * HEAD] = dot(prob.astype(BF), pj[:, base + 2 * HEAD:base + 3 * HEAD]).astype(BF)

    def head_backward(h):
        base = h * 3 * HEAD
        value = pj[:, base + 2 * HEAD:base + 3 * HEAD]
        incoming = ga[:, h * HEAD:(h + 1) * HEAD]
        prob = probs[h]
        gp[:, base + 2 * HEAD:base + 3 * HEAD] = dot_tn(prob.astype(BF), incoming).astype(BF)
        grad_probs = dot_nt(incoming, value)
        grad_scores = (prob * (grad_probs - jnp.sum(prob * grad_probs, axis=-1, keepdims=True)) * SCALE).astype(BF)
        query, query_inv = head_norm(pj[:, base:base + HEAD].astype(F32))
        keys, key_inv = head_norm(pj[:, base + HEAD:base + 2 * HEAD].astype(F32))
        grad_qn = dot(grad_scores, kb[h])
        grad_kn = dot_tn(grad_scores, qb[h])
        gp[:, base:base + HEAD] = head_norm_back(grad_qn, query, query_inv, qg_ref[...]).astype(BF)
        gp[:, base + HEAD:base + 2 * HEAD] = head_norm_back(grad_kn, keys, key_inv, kg_ref[...]).astype(BF)

    def make_terms(group, left, weights, terms):
        @pl.loop(0, (5, 4, 7)[group])
        def _(i):
            if group == 0:
                late = i // 3
                dy = (1 - late) * 2 + late * (2 * i - 5)
                dz = (1 - late) * (i + 1) + late * 2
            elif group == 1:
                dy, dz = 1 + 2 * (i // 2), 1 + 2 * (i % 2)
            else:
                late = i // 4
                dy, dz = late * (i - 3), (1 - late) * i
            block = ((y + dy) % RING) * RING + (z + dz) % RING
            at = pl.ds(pl.multiple_of(block * FEAT, 128), FEAT)
            value = dot_nt(left[...], weights[at, :]).astype(BF)
            terms[:, pl.ds(pl.multiple_of((dy * RING + dz) * FEAT, 128), FEAT)] = value

    project(0, 4)
    gather_g.forward2(0)
    project(4, 8)
    gather_g.forward2(1)
    pj[...] = qkv_ref[0:ROWS, :].astype(BF)
    head_forward(0)
    gather_g.forward2(-1)
    head_forward(1)
    load_o.wait()
    make_terms(0, att, wo, term)
    gather_g.forward2(2)
    scatter_p.send(2)
    make_terms(1, att, wo, term)
    scatter_p.send(1)
    scatter_p.send(3)
    make_terms(2, att, wo, term)
    scatter_p.send(0)
    gather_g.finish()

    def grad_attended():
        @pl.loop(0, 8)
        def _(k):
            at = pl.ds(pl.multiple_of(k * 768, 768), 768)
            part = dot(gf[:, at], wo[at, :])

            @pl.when(k == 0)
            def _():
                qkv_ref[0:ROWS, 0:OUT] = part

            @pl.when(k > 0)
            def _():
                qkv_ref[0:ROWS, 0:OUT] += part

        ga[...] = qkv_ref[0:ROWS, 0:OUT].astype(BF)

    grad_o.send(2)
    grad_o.send(1)
    grad_o.add(2)
    scatter_p.pass_on(2)
    grad_attended()
    grad_o.send(3)
    grad_o.add(1)
    grad_o.add(3)
    scatter_p.pass_on(1)
    head_backward(0)
    scatter_p.pass_on(3)
    head_backward(1)
    grad_q.send(2)
    scatter_p.pass_on(0)
    grad_o.send(0)
    grad_q.send(1)
    grad_q.add(2)
    grad_o.add(0)
    grad_o.ring.pass_on()
    scatter_p.collect(2)
    settle(gather_g.copies())
    make_terms(0, gp, wq, gf)
    scatter_b.send(2)
    scatter_p.collect(1)
    scatter_p.collect(3)
    make_terms(1, gp, wq, gf)
    scatter_b.send(1)
    scatter_b.send(3)
    scatter_p.last_pass()
    make_terms(2, gp, wq, gf)
    scatter_b.send(0)
    scatter_p.collect(0)
    grad_q.add(1)
    grad_q.send(3)
    scatter_b.pass_on(2)
    for h in (0, 1):
        rows = pl.ds(h * HALF, HALF)
        live = lax.broadcasted_iota(jnp.int32, (HALF, FEAT), 0) + h * HALF < total_rows
        value = own_x[rows, :].astype(F32) + scatter_p.result(h)
        block_ref[rows, :] = jnp.where(live, value, 0.0).astype(BF)
    saved(pltpu.make_async_copy(block_ref, block_hbm, lsem.at[2]))
    scatter_b.pass_on(1)
    scatter_b.pass_on(3)
    grad_q.add(3)
    scatter_b.pass_on(0)
    grad_q.send(0)
    grad_q.ring.pass_on()
    scatter_b.collect(2)
    grad_q.add(0)
    scatter_b.collect(1)
    scatter_b.collect(3)
    grad_o.finish()
    saved(pltpu.make_async_copy(out_ref, out_hbm, lsem.at[3]))
    scatter_b.last_pass()
    scatter_b.collect(0)
    for h in (0, 1):
        rows = pl.ds(h * HALF, HALF)
        own_g[rows, :] = (own_g[rows, :].astype(F32) + scatter_b.result(h)).astype(BF)
    og2[...] = dot_tn(pack[...], own_g[...]).astype(BF)
    for copy in swap_g:
        start(copy)
    ar2[here, :] = og2[here, :]
    grad_q.finish()
    saved(pltpu.make_async_copy(qkv_ref, qkv_hbm, lsem.at[4]))
    for copy in swap_g:
        copy.wait_recv()
    pgrad_ref[...] = dot(sel_t[...], ar2[...]).astype(BF)
    saved(pltpu.make_async_copy(pgrad_ref, pgrad_hbm, lsem.at[5]))
    grad_q.close()
    grad_o.close()
    settle(list(sent.values()))
    for copy in saves:
        copy.wait()


def hand_over(*refs):
    inputs, outputs, held, sems = refs[:4], refs[4:8], refs[8:12], refs[12]
    pairs = []
    for source, target, stage in zip(inputs, outputs, held):
        pieces = max(1, source.shape[0] * source.shape[1] // (192 * 768))
        step = source.shape[0] // pieces
        for p in range(pieces):
            at = pl.ds(p * step, step)
            k = len(pairs)
            pairs.append((
                pltpu.make_async_copy(source.at[at], stage.at[at], sems.at[0, k]),
                pltpu.make_async_copy(stage.at[at], target.at[at], sems.at[1, k]),
            ))
    for fetch, _ in pairs:
        fetch.start()
    for fetch, store in pairs:
        fetch.wait()
        store.start()
    for _, store in pairs:
        store.wait()


def shards(
    patches, keep_index, keep_count, pack_dest, pack_offset, w_qkv, q_gain, k_gain, w_out, cotangent
):
    vmem = pl.BlockSpec(memory_space=pltpu.VMEM)
    hbm = pl.BlockSpec(memory_space=pltpu.HBM)
    smem = pl.BlockSpec(memory_space=pltpu.SMEM)
    results = (
        jax.ShapeDtypeStruct((ROWS, FEAT), BF),
        jax.ShapeDtypeStruct((ROWS, FEAT), BF),
        jax.ShapeDtypeStruct((GRAD_ROWS, QKV), F32),
        jax.ShapeDtypeStruct((GRAD_ROWS, OUT), F32),
    )
    done = pl.pallas_call(
        kernel,
        out_shape=results,
        in_specs=[smem] * 3 + [vmem] * 5 + [hbm] * 2,
        out_specs=(hbm,) * 4,
        scratch_shapes=[
            *(pltpu.VMEM(r.shape, r.dtype) for r in results),
            pltpu.VMEM((D, QKV), BF),
            pltpu.VMEM((D, OUT), BF),
            pltpu.VMEM((ROWS, D), BF),
            pltpu.VMEM((ROWS, D), BF),
            pltpu.VMEM((ROWS, D), BF),
            pltpu.VMEM((ROWS, QKV), BF),
            pltpu.VMEM((ROWS, QKV), BF),
            pltpu.VMEM((ROWS, OUT), BF),
            pltpu.VMEM((ROWS, OUT), BF),
            pltpu.VMEM((HEADS_DEV, ROWS, HEAD), BF),
            pltpu.VMEM((HEADS_DEV, ROWS, HEAD), BF),
            pltpu.VMEM((HEADS_DEV, ROWS, ROWS), F32),
            pltpu.VMEM((ROWS, ROWS), F32),
            pltpu.VMEM((ROWS, ROWS), BF),
            pltpu.VMEM((ROWS, ROWS), BF),
            pltpu.VMEM((ROWS, FEAT), BF),
            pltpu.VMEM((ROWS, FEAT), BF),
            pltpu.VMEM((ROWS, FEAT), BF),
            pltpu.VMEM((ROWS, FEAT), BF),
            pltpu.VMEM((ROWS, FEAT), BF),
            pltpu.VMEM((ROWS, FEAT), BF),
            pltpu.VMEM((2, RING + 1, 3 * HALF, FEAT), BF),
            pltpu.VMEM((2, RING + 1, 3 * HALF, FEAT), BF),
            pltpu.VMEM((2, GRAD_ROWS, QKV), BF),
            pltpu.VMEM((RING, GRAD_ROWS, QKV), BF),
            pltpu.VMEM((3 * GRAD_ROWS, QKV), BF),
            pltpu.VMEM((4, GRAD_ROWS, OUT), BF),
            pltpu.VMEM((RING, GRAD_ROWS, OUT), BF),
            pltpu.VMEM((3 * GRAD_ROWS, OUT), BF),
            pltpu.SemaphoreType.DMA((N_SEMS,)),
            pltpu.SemaphoreType.DMA((N_SEMS,)),
            pltpu.SemaphoreType.DMA((6,)),
        ],
        compiler_params=pltpu.CompilerParams(
            collective_id=0, has_side_effects=True, vmem_limit_bytes=63 << 20
        ),
        cost_estimate=pl.CostEstimate(flops=15_000_000_000, bytes_accessed=20_000_000, transcendentals=300_000),
        name="block",
    )(
        keep_count, pack_dest, pack_offset, keep_index, q_gain.reshape(1, HEAD), k_gain.reshape(1, HEAD),
        patches, cotangent, w_qkv, w_out,
    )
    return pl.pallas_call(
        hand_over,
        out_shape=results,
        in_specs=[hbm] * 4,
        out_specs=(hbm,) * 4,
        scratch_shapes=[
            *(pltpu.VMEM(r.shape, r.dtype) for r in results),
            pltpu.SemaphoreType.DMA((2, 8)),
        ],
        name="hand_over",
    )(*done)


def solution(mesh):
    placed = (
        P("dp", "mp"), P("dp", None), P(), P(), P(), P(None, "mp"), P(), P(), P(None, "mp"), P("dp", "mp"),
    )
    return jax.shard_map(
        shards, mesh=mesh, in_specs=placed, out_specs=(P("dp", "mp"),) * 4, check_vma=False,
    )
```

```python
import functools

import jax
import jax.numpy as jnp
from jax import lax
from jax.experimental import pallas as pl
from jax.experimental.pallas import tpu as pltpu
from jax.sharding import PartitionSpec as P

MESH = pl.DeviceIdType.MESH
BF, F32 = jnp.bfloat16, jnp.float32
N_DP, RING = 8, 4
ROWS = 384
SLOTS = 48
FEAT = 384
D = 6144
HEAD = 128
HEADS_DEV = 2
QKV = 3 * HEAD * HEADS_DEV
OUT = HEAD * HEADS_DEV
GRAD_ROWS = D // N_DP
HALF, QUART = ROWS // 2, ROWS // 4
EPSILON = 1e-06
SCALE = HEAD ** (-0.5)
N_SEMS = 256


def dot(a, b):
    return jnp.dot(a, b, preferred_element_type=F32)


def dot_nt(a, b):
    return lax.dot_general(a, b, (((1,), (1,)), ((), ())), preferred_element_type=F32)


def dot_tn(a, b):
    return lax.dot_general(a, b, (((0,), (0,)), ((), ())), preferred_element_type=F32)


def head_norm(values):
    centred = values - jnp.mean(values, axis=-1, keepdims=True)
    variance = jnp.mean(centred * centred, axis=-1, keepdims=True)
    inverse = lax.rsqrt(variance + EPSILON)
    return centred * inverse, inverse


def head_norm_back(incoming, normed, inverse, gain):
    scaled = incoming * gain
    return (
        scaled
        - jnp.mean(scaled, axis=-1, keepdims=True)
        - normed * jnp.mean(scaled * normed, axis=-1, keepdims=True)
    ) * inverse


def kernel(
    count_hbm, dest_hbm, offset_hbm, keep_hbm, qg_hbm, kg_hbm, patches_hbm, cot_hbm, wq_hbm, wo_hbm,
    block_hbm, pgrad_hbm, qkv_hbm, out_hbm,
    count_ref, dest_ref, offset_ref, keep_ref, qg_ref, kg_ref, patches_ref, cot_ref,
    block_ref, pgrad_ref, qkv_ref, out_ref,
    wq, wo, xf, gf, term, pj, gp, att, ga, qb, kb, probs, bias, sel_t, pack, own_x, own_g,
    og, ar, og2, ar2, rb1, rb2, pq, cq, rq, po, co, ro, ssem, rsem, lsem,
):
    dp, mp = lax.axis_index("dp"), lax.axis_index("mp")
    x, c = dp // 2, dp % 2
    y, z = mp // RING, mp % RING
    counter = [0]

    def at_mp(yy, zz):
        return (dp, (yy % RING) * RING + zz % RING)

    def at_dp(xx, cc):
        return ((xx % RING) * 2 + cc, mp)

    def along(axis, step):
        if axis == "y":
            return at_mp(y + RING + step, z)
        if axis == "z":
            return at_mp(y, z + RING + step)
        return at_dp(x + RING + step, c)

    def remote(src, dst, device):
        k = counter[0]
        counter[0] += 1
        return pltpu.make_async_remote_copy(
            src_ref=src, dst_ref=dst, send_sem=ssem.at[k], recv_sem=rsem.at[k],
            device_id=device, device_id_type=MESH,
        )

    sent = {}

    def start(copy):
        copy.start()
        sent[id(copy)] = copy

    def settle(copies):
        for copy in copies:
            sent.pop(id(copy)).wait_send()

    def column(dy, dz):
        block = ((y + dy) % RING) * RING + (z + dz) % RING
        return pl.ds(pl.multiple_of(block * FEAT, 128), FEAT)

    class Gather:
        def __init__(self, full):
            self.full = full
            self.one, self.fwd, self.two, self.fwd2 = {}, {}, {}, {}
            for h in (0, 1):
                a, b = ("y", "z") if h == 0 else ("z", "y")
                for s in (1, -1):
                    self.one[h, s] = self.copy(h, 0, 0, 0, HALF, a, s)
                    self.fwd[h, s] = self.copy(h, -s, 0, 0 if s == 1 else QUART, QUART, a, s)
                    for da in (0, 1, -1, 2):
                        self.two[h, da, s] = self.copy(h, da, 0, 0, HALF, b, s)
                        self.fwd2[h, da, s] = self.copy(h, da, -s, 0 if s == 1 else QUART, QUART, b, s)

        def copy(self, h, da, db, low, n, axis, s):
            dy, dz = (da, db) if h == 0 else (db, da)
            ref = self.full.at[pl.ds(h * HALF + low, n), column(dy + RING, dz + RING)]
            return remote(ref, ref, along(axis, s))

        def begin(self):
            for s in (1, -1):
                for h in (0, 1):
                    start(self.one[h, s])

        def second(self, da):
            for s in (1, -1):
                for h in (0, 1):
                    start(self.two[h, da, s])

        def forward(self, then=True):
            for s in (1, -1):
                for h in (0, 1):
                    self.one[h, s].wait_recv()
                    start(self.fwd[h, s])
            if then:
                self.second(1)
                self.second(-1)

        def opposite(self):
            for s in (1, -1):
                for h in (0, 1):
                    self.fwd[h, s].wait_recv()

        def forward2(self, da):
            for s in (1, -1):
                for h in (0, 1):
                    self.two[h, da, s].wait_recv()
                    start(self.fwd2[h, da, s])

        def copies(self):
            return [copy for group in (self.one, self.fwd, self.two, self.fwd2) for copy in group.values()]

        def finish(self, das=(0, 1, -1, 2)):
            for da in das:
                for s in (1, -1):
                    for h in (0, 1):
                        self.fwd2[h, da, s].wait_recv()

    class Ring:
        def __init__(self, part, box, rows, axis, chunk=None):
            half = rows // 2
            self.part, self.box, self.rows, self.half = part, box, rows, half
            self.chunk = chunk
            self.c0 = remote(part(2, 0, half), box(0, half), along(axis, 1))
            self.c1 = remote(part(2, half, half), box(half, half), along(axis, -1))
            self.c2 = remote(part(1, half, half), box(rows + half, half), along(axis, 1))
            self.c3 = remote(part(3, 0, half), box(2 * rows, half), along(axis, -1))
            self.c4 = remote(part(1, 0, half), box(rows, half), along(axis, 1))
            self.c5 = remote(part(3, half, half), box(2 * rows + half, half), along(axis, -1))

        def far(self):
            start(self.c0)
            start(self.c1)

        def near(self):
            start(self.c2)
            start(self.c3)

        def add(self, r, low, box_low):
            if self.chunk is None:
                ref = self.part(r, low, self.half)
                ref[...] = (ref[...].astype(F32) + self.box(box_low, self.half)[...].astype(F32)).astype(BF)
                return

            @pl.loop(0, self.half // self.chunk)
            def _(i):
                step = pl.multiple_of(i * self.chunk, self.chunk)
                ref = self.part(r, low + step, self.chunk)
                ref[...] = (ref[...].astype(F32) + self.box(box_low + step, self.chunk)[...].astype(F32)).astype(BF)

        def pass_on(self):
            self.c0.wait_recv()
            self.add(1, 0, 0)
            start(self.c4)
            self.c1.wait_recv()
            self.add(3, self.half, self.half)
            start(self.c5)

        def arrive(self):
            for copy in (self.c2, self.c3, self.c4, self.c5):
                copy.wait_recv()

        def total(self, low, n):
            return (
                self.part(0, low, n)[...].astype(F32)
                + self.box(self.rows + low, n)[...].astype(F32)
                + self.box(2 * self.rows + low, n)[...].astype(F32)
            )

    class Scatter:
        def __init__(self, terms, boxes):
            self.first, self.last = {}, {}
            for h in (0, 1):
                a, b = ("z", "y") if h == 0 else ("y", "z")

                def piece(r1, r2, low, n, h=h):
                    slot = r2 * RING + r1 if h == 0 else r1 * RING + r2
                    return terms.at[pl.ds(h * HALF + low, n), pl.ds(slot * FEAT, FEAT)]

                for r2 in range(RING):
                    self.first[h, r2] = Ring(
                        lambda r, low, n, r2=r2, piece=piece: piece(r, r2, low, n),
                        lambda low, n, h=h, r2=r2: boxes.at[h, r2, pl.ds(low, n)],
                        HALF, a,
                    )
                self.last[h] = Ring(
                    lambda r, low, n, piece=piece: piece(0, r, low, n),
                    lambda low, n, h=h: boxes.at[h, RING, pl.ds(low, n)],
                    HALF, b,
                )

        def send(self, r2):
            for h in (0, 1):
                self.first[h, r2].far()
            for h in (0, 1):
                self.first[h, r2].near()

        def pass_on(self, r2):
            for h in (0, 1):
                self.first[h, r2].pass_on()

        def collect(self, r2):
            for h in (0, 1):
                ring = self.first[h, r2]
                ring.arrive()
                ring.part(0, 0, HALF)[...] = ring.total(0, HALF).astype(BF)
                if r2 == 2:
                    self.last[h].far()
            if r2 == 3:
                for h in (0, 1):
                    self.last[h].near()

        def last_pass(self):
            for h in (0, 1):
                self.last[h].pass_on()

        def result(self, h):
            self.last[h].arrive()
            return self.last[h].total(0, HALF)

    class WeightGrad:
        def __init__(self, rows, cols, width, mine, theirs, boxes, slots, result):
            self.rows, self.cols, self.mine, self.theirs, self.result = rows, cols, mine, theirs, result
            self.slots = slots
            self.swap = {
                dx: remote(mine.at[i % slots], theirs.at[dx], at_dp(x, 1 - c)) for i, dx in enumerate((2, 1, 3, 0))
            }
            self.ring = Ring(
                lambda r, low, n: theirs.at[r, pl.ds(low, n)], lambda low, n: boxes.at[pl.ds(low, n)],
                GRAD_ROWS, "x", chunk=64,
            )
            self.order = []

        def tile(self, dx, core, m):
            block = ((x + dx) % RING) * 2 + core
            left = self.rows[:, pl.ds(pl.multiple_of(block * GRAD_ROWS + m * 256, 128), 256)]
            return dot_tn(left, self.cols[...])

        def send(self, dx):
            i = len(self.order)
            if i >= self.slots:
                self.swap[self.order[i - self.slots]].wait_send()
            self.order.append(dx)
            slot = i % self.slots

            @pl.loop(0, GRAD_ROWS // 256)
            def _(m):
                self.mine[slot, pl.ds(pl.multiple_of(m * 256, 256), 256), :] = self.tile(dx, 1 - c, m).astype(BF)

            self.swap[dx].start()

        def add(self, dx):
            self.swap[dx].wait_recv()

            @pl.loop(0, GRAD_ROWS // 256)
            def _(m):
                at = pl.ds(pl.multiple_of(m * 256, 256), 256)
                value = self.tile(dx, c, m) + self.theirs[dx, at, :].astype(F32)
                if dx == 0:
                    self.result[at, :] = value
                else:
                    self.theirs[dx, at, :] = value.astype(BF)

            if dx == 2:
                self.ring.far()
            if dx == 3:
                self.ring.near()

        def finish(self):
            self.ring.arrive()

            @pl.loop(0, GRAD_ROWS // 64)
            def _(i):
                low = pl.multiple_of(i * 64, 64)
                at = pl.ds(low, 64)
                self.result[at, :] = (
                    self.result[at, :]
                    + self.ring.box(GRAD_ROWS + low, 64)[...].astype(F32)
                    + self.ring.box(2 * GRAD_ROWS + low, 64)[...].astype(F32)
                )

        def close(self):
            for dx in self.order[-self.slots:]:
                self.swap[dx].wait_send()

    loads = [
        pltpu.make_async_copy(source, target, lsem.at[6 + i])
        for i, (source, target) in enumerate((
            (count_hbm, count_ref), (dest_hbm, dest_ref), (offset_hbm, offset_ref), (keep_hbm, keep_ref),
            (cot_hbm, cot_ref), (patches_hbm, patches_ref), (qg_hbm, qg_ref), (kg_hbm, kg_ref),
        ))
    ]
    for copy in loads:
        copy.start()
    load_q = pltpu.make_async_copy(wq_hbm, wq, lsem.at[0])
    load_o = pltpu.make_async_copy(wo_hbm, wo, lsem.at[1])

    barrier = pltpu.get_barrier_semaphore()
    for axis in ("y", "z"):
        for s in (1, -1):
            pl.semaphore_signal(barrier, inc=1, device_id=along(axis, s), device_id_type=MESH)
    for o in range(1, N_DP):
        pl.semaphore_signal(barrier, inc=1, device_id=((dp + o) % N_DP, mp), device_id_type=MESH)

    load_q.start()
    load_o.start()

    def saved(copy):
        copy.start()
        saves.append(copy)

    saves = []
    for copy in loads:
        copy.wait()
    lane = lax.broadcasted_iota(jnp.int32, (1, ROWS), 1)
    part = (lane * 1366) >> 16
    slot = lane - part * SLOTS
    off = jnp.full((1, ROWS), -1, jnp.int32)
    total_rows = 0
    for t in range(N_DP):
        base, here_count = 0, 0
        for k in range(N_DP):
            mine = dest_ref[t * N_DP + k] == dp
            base += jnp.where(mine, offset_ref[t * N_DP + k], 0)
            here_count += jnp.where(mine, count_ref[t * N_DP + k], 0)
        off = jnp.where((part == t) & (slot < here_count), base + slot, off)
        total_rows += here_count
    spread_row = lax.broadcasted_iota(jnp.int32, (SLOTS, ROWS), 0)
    spread = (spread_row == slot).astype(F32).astype(BF)
    kept = dot(keep_ref[...].astype(F32).astype(BF), spread).astype(jnp.int32)
    src = jnp.full((1, ROWS), -1, jnp.int32)
    for k in range(N_DP):
        goes = (part == dest_ref[dp * N_DP + k]) & (slot < count_ref[dp * N_DP + k])
        src = jnp.where(goes, kept[k:k + 1, :] + k * SLOTS, src)
    row_id = lax.broadcasted_iota(jnp.int32, (ROWS, ROWS), 0)
    col_id = lax.broadcasted_iota(jnp.int32, (ROWS, ROWS), 1)
    row_live = row_id < total_rows
    col_live = col_id < total_rows
    own_g[...] = jnp.where(row_live, cot_ref[...].astype(F32), 0.0).astype(BF)
    gf[:, column(0, 0)] = own_g[...]
    sel_t[...] = (row_id == src).astype(F32).astype(BF)
    og[...] = dot_tn(sel_t[...], patches_ref[...]).astype(BF)

    gather_g, gather_x = Gather(gf), Gather(xf)
    swap_x = [
        remote(og.at[pl.ds(pl.multiple_of(((dp + o) % N_DP) * SLOTS, SLOTS), SLOTS)],
               ar.at[pl.ds(pl.multiple_of(dp * SLOTS, SLOTS), SLOTS)], ((dp + o) % N_DP, mp))
        for o in range(1, N_DP)
    ]
    swap_g = [
        remote(og2.at[pl.ds(pl.multiple_of(((dp + o) % N_DP) * SLOTS, SLOTS), SLOTS)],
               ar2.at[pl.ds(pl.multiple_of(dp * SLOTS, SLOTS), SLOTS)], ((dp + o) % N_DP, mp))
        for o in range(1, N_DP)
    ]
    scatter_p, scatter_b = Scatter(term, rb1), Scatter(gf, rb2)
    grad_q = WeightGrad(xf, gp, QKV, pq, cq, rq, 2, qkv_ref)
    grad_o = WeightGrad(gf, att, OUT, po, co, ro, 4, out_ref)
    assert counter[0] <= N_SEMS

    pl.semaphore_wait(barrier, 4 + N_DP - 1)
    for copy in swap_x:
        start(copy)
    gather_g.begin()
    gather_g.second(0)
    here = pl.ds(pl.multiple_of(dp * SLOTS, SLOTS), SLOTS)
    ar[here, :] = og[here, :]
    pack[...] = (row_id == off).astype(F32).astype(BF)
    for copy in swap_x:
        copy.wait_recv()
    own_x[...] = dot(pack[...], ar[...]).astype(BF)
    xf[:, column(0, 0)] = own_x[...]
    gather_x.begin()
    gather_x.second(0)
    gather_g.forward(then=False)
    gather_x.forward()
    gather_g.opposite()
    gather_x.opposite()
    gather_x.second(2)
    same = ((row_id * 1366) >> 16) == ((col_id * 1366) >> 16)
    image = dot(pack[...], same.astype(F32).astype(BF)).astype(BF)
    both = dot_nt(image, pack[...]) > 0.5
    bias[...] = jnp.where(both | (jnp.logical_not(row_live) & jnp.logical_not(col_live)), 0.0, -jnp.inf)
    for da in (0, 1, -1):
        gather_x.forward2(da)
    gather_g.forward2(0)
    gather_x.forward2(2)
    for da in (1, -1, 2):
        gather_g.second(da)
    gather_x.finish()
    load_q.wait()

    def project(low, high):
        @pl.loop(low, high)
        def _(k):
            at = pl.ds(pl.multiple_of(k * 768, 768), 768)
            part = dot(xf[:, at], wq[at, :])

            @pl.when(k == 0)
            def _():
                qkv_ref[0:ROWS, :] = part

            @pl.when(k > 0)
            def _():
                qkv_ref[0:ROWS, :] += part

    def head_forward(h):
        base = h * 3 * HEAD
        query, _ = head_norm(pj[:, base:base + HEAD].astype(F32))
        keys, _ = head_norm(pj[:, base + HEAD:base + 2 * HEAD].astype(F32))
        qb[h] = (query * qg_ref[...]).astype(BF)
        kb[h] = (keys * kg_ref[...]).astype(BF)
        scores = dot_nt(qb[h], kb[h]) * SCALE + bias[...]
        exponent = jnp.exp(scores - jnp.max(scores, axis=-1, keepdims=True))
        prob = exponent / jnp.sum(exponent, axis=-1, keepdims=True)
        probs[h] = prob
        att[:, h * HEAD:(h + 1) * HEAD] = dot(prob.astype(BF), pj[:, base + 2 * HEAD:base + 3 * HEAD]).astype(BF)

    def head_backward(h):
        base = h * 3 * HEAD
        value = pj[:, base + 2 * HEAD:base + 3 * HEAD]
        incoming = ga[:, h * HEAD:(h + 1) * HEAD]
        prob = probs[h]
        gp[:, base + 2 * HEAD:base + 3 * HEAD] = dot_tn(prob.astype(BF), incoming).astype(BF)
        grad_probs = dot_nt(incoming, value)
        grad_scores = (prob * (grad_probs - jnp.sum(prob * grad_probs, axis=-1, keepdims=True)) * SCALE).astype(BF)
        query, query_inv = head_norm(pj[:, base:base + HEAD].astype(F32))
        keys, key_inv = head_norm(pj[:, base + HEAD:base + 2 * HEAD].astype(F32))
        grad_qn = dot(grad_scores, kb[h])
        grad_kn = dot_tn(grad_scores, qb[h])
        gp[:, base:base + HEAD] = head_norm_back(grad_qn, query, query_inv, qg_ref[...]).astype(BF)
        gp[:, base + HEAD:base + 2 * HEAD] = head_norm_back(grad_kn, keys, key_inv, kg_ref[...]).astype(BF)

    def make_terms(group, left, weights, terms):
        @pl.loop(0, (5, 4, 7)[group])
        def _(i):
            if group == 0:
                late = i // 3
                dy = (1 - late) * 2 + late * (2 * i - 5)
                dz = (1 - late) * (i + 1) + late * 2
            elif group == 1:
                dy, dz = 1 + 2 * (i // 2), 1 + 2 * (i % 2)
            else:
                late = i // 4
                dy, dz = late * (i - 3), (1 - late) * i
            block = ((y + dy) % RING) * RING + (z + dz) % RING
            at = pl.ds(pl.multiple_of(block * FEAT, 128), FEAT)
            value = dot_nt(left[...], weights[at, :]).astype(BF)
            terms[:, pl.ds(pl.multiple_of((dy * RING + dz) * FEAT, 128), FEAT)] = value

    project(0, 8)
    gather_g.forward2(1)
    pj[...] = qkv_ref[0:ROWS, :].astype(BF)
    head_forward(0)
    gather_g.forward2(-1)
    head_forward(1)
    load_o.wait()
    make_terms(0, att, wo, term)
    gather_g.forward2(2)
    scatter_p.send(2)
    make_terms(1, att, wo, term)
    scatter_p.send(1)
    scatter_p.send(3)
    make_terms(2, att, wo, term)
    scatter_p.send(0)
    gather_g.finish()

    def grad_attended():
        @pl.loop(0, 8)
        def _(k):
            at = pl.ds(pl.multiple_of(k * 768, 768), 768)
            part = dot(gf[:, at], wo[at, :])

            @pl.when(k == 0)
            def _():
                qkv_ref[0:ROWS, 0:OUT] = part

            @pl.when(k > 0)
            def _():
                qkv_ref[0:ROWS, 0:OUT] += part

        ga[...] = qkv_ref[0:ROWS, 0:OUT].astype(BF)

    grad_o.send(2)
    grad_o.send(1)
    grad_o.add(2)
    scatter_p.pass_on(2)
    grad_attended()
    grad_o.send(3)
    grad_o.add(1)
    grad_o.add(3)
    scatter_p.pass_on(1)
    head_backward(0)
    scatter_p.pass_on(3)
    head_backward(1)
    grad_q.send(2)
    grad_q.send(1)
    grad_q.add(2)
    scatter_p.pass_on(0)
    grad_q.send(3)
    grad_o.ring.pass_on()
    grad_q.add(1)
    grad_o.send(0)
    grad_q.add(3)
    scatter_p.collect(2)
    grad_o.add(0)
    settle(gather_g.copies())
    make_terms(0, gp, wq, gf)
    scatter_b.send(2)
    scatter_p.collect(1)
    scatter_p.collect(3)
    make_terms(1, gp, wq, gf)
    scatter_b.send(1)
    scatter_b.send(3)
    scatter_p.last_pass()
    make_terms(2, gp, wq, gf)
    scatter_b.send(0)
    scatter_p.collect(0)
    scatter_b.pass_on(2)
    grad_q.send(0)
    grad_q.ring.pass_on()
    scatter_b.pass_on(1)
    scatter_b.pass_on(3)
    for h in (0, 1):
        rows = pl.ds(h * HALF, HALF)
        live = lax.broadcasted_iota(jnp.int32, (HALF, FEAT), 0) + h * HALF < total_rows
        value = own_x[rows, :].astype(F32) + scatter_p.result(h)
        block_ref[rows, :] = jnp.where(live, value, 0.0).astype(BF)
    saved(pltpu.make_async_copy(block_ref, block_hbm, lsem.at[2]))
    scatter_b.pass_on(0)
    scatter_b.collect(2)
    grad_q.add(0)
    scatter_b.collect(1)
    scatter_b.collect(3)
    grad_o.finish()
    saved(pltpu.make_async_copy(out_ref, out_hbm, lsem.at[3]))
    scatter_b.last_pass()
    scatter_b.collect(0)
    for h in (0, 1):
        rows = pl.ds(h * HALF, HALF)
        own_g[rows, :] = (own_g[rows, :].astype(F32) + scatter_b.result(h)).astype(BF)
    og2[...] = dot_tn(pack[...], own_g[...]).astype(BF)
    for copy in swap_g:
        start(copy)
    ar2[here, :] = og2[here, :]
    grad_q.finish()
    saved(pltpu.make_async_copy(qkv_ref, qkv_hbm, lsem.at[4]))
    for copy in swap_g:
        copy.wait_recv()
    pgrad_ref[...] = dot(sel_t[...], ar2[...]).astype(BF)
    saved(pltpu.make_async_copy(pgrad_ref, pgrad_hbm, lsem.at[5]))
    grad_q.close()
    grad_o.close()
    settle(list(sent.values()))
    for copy in saves:
        copy.wait()


def hand_over(*refs):
    inputs, outputs, held, sems = refs[:4], refs[4:8], refs[8:12], refs[12]
    pairs = []
    for source, target, stage in zip(inputs, outputs, held):
        pieces = max(1, source.shape[0] * source.shape[1] // (192 * 768))
        step = source.shape[0] // pieces
        for p in range(pieces):
            at = pl.ds(p * step, step)
            k = len(pairs)
            pairs.append((
                pltpu.make_async_copy(source.at[at], stage.at[at], sems.at[0, k]),
                pltpu.make_async_copy(stage.at[at], target.at[at], sems.at[1, k]),
            ))
    for fetch, _ in pairs:
        fetch.start()
    for fetch, store in pairs:
        fetch.wait()
        store.start()
    for _, store in pairs:
        store.wait()


def shards(
    patches, keep_index, keep_count, pack_dest, pack_offset, w_qkv, q_gain, k_gain, w_out, cotangent
):
    hbm = pl.BlockSpec(memory_space=pltpu.HBM)
    results = (
        jax.ShapeDtypeStruct((ROWS, FEAT), BF),
        jax.ShapeDtypeStruct((ROWS, FEAT), BF),
        jax.ShapeDtypeStruct((GRAD_ROWS, QKV), F32),
        jax.ShapeDtypeStruct((GRAD_ROWS, OUT), F32),
    )
    done = pl.pallas_call(
        kernel,
        out_shape=results,
        in_specs=[hbm] * 10,
        out_specs=(hbm,) * 4,
        scratch_shapes=[
            pltpu.SMEM((N_DP * N_DP,), jnp.int32),
            pltpu.SMEM((N_DP * N_DP,), jnp.int32),
            pltpu.SMEM((N_DP * N_DP,), jnp.int32),
            pltpu.VMEM((N_DP, SLOTS), jnp.int32),
            pltpu.VMEM((1, HEAD), F32),
            pltpu.VMEM((1, HEAD), F32),
            pltpu.VMEM((ROWS, FEAT), BF),
            pltpu.VMEM((ROWS, FEAT), BF),
            *(pltpu.VMEM(r.shape, r.dtype) for r in results),
            pltpu.VMEM((D, QKV), BF),
            pltpu.VMEM((D, OUT), BF),
            pltpu.VMEM((ROWS, D), BF),
            pltpu.VMEM((ROWS, D), BF),
            pltpu.VMEM((ROWS, D), BF),
            pltpu.VMEM((ROWS, QKV), BF),
            pltpu.VMEM((ROWS, QKV), BF),
            pltpu.VMEM((ROWS, OUT), BF),
            pltpu.VMEM((ROWS, OUT), BF),
            pltpu.VMEM((HEADS_DEV, ROWS, HEAD), BF),
            pltpu.VMEM((HEADS_DEV, ROWS, HEAD), BF),
            pltpu.VMEM((HEADS_DEV, ROWS, ROWS), F32),
            pltpu.VMEM((ROWS, ROWS), F32),
            pltpu.VMEM((ROWS, ROWS), BF),
            pltpu.VMEM((ROWS, ROWS), BF),
            pltpu.VMEM((ROWS, FEAT), BF),
            pltpu.VMEM((ROWS, FEAT), BF),
            pltpu.VMEM((ROWS, FEAT), BF),
            pltpu.VMEM((ROWS, FEAT), BF),
            pltpu.VMEM((ROWS, FEAT), BF),
            pltpu.VMEM((ROWS, FEAT), BF),
            pltpu.VMEM((2, RING + 1, 3 * HALF, FEAT), BF),
            pltpu.VMEM((2, RING + 1, 3 * HALF, FEAT), BF),
            pltpu.VMEM((2, GRAD_ROWS, QKV), BF),
            pltpu.VMEM((RING, GRAD_ROWS, QKV), BF),
            pltpu.VMEM((3 * GRAD_ROWS, QKV), BF),
            pltpu.VMEM((4, GRAD_ROWS, OUT), BF),
            pltpu.VMEM((RING, GRAD_ROWS, OUT), BF),
            pltpu.VMEM((3 * GRAD_ROWS, OUT), BF),
            pltpu.SemaphoreType.DMA((N_SEMS,)),
            pltpu.SemaphoreType.DMA((N_SEMS,)),
            pltpu.SemaphoreType.DMA((14,)),
        ],
        compiler_params=pltpu.CompilerParams(
            collective_id=0, has_side_effects=True, vmem_limit_bytes=63 << 20
        ),
        cost_estimate=pl.CostEstimate(flops=15_000_000_000, bytes_accessed=20_000_000, transcendentals=300_000),
        name="block",
    )(
        keep_count, pack_dest, pack_offset, keep_index, q_gain.reshape(1, HEAD), k_gain.reshape(1, HEAD),
        patches, cotangent, w_qkv, w_out,
    )
    return pl.pallas_call(
        hand_over,
        out_shape=results,
        in_specs=[hbm] * 4,
        out_specs=(hbm,) * 4,
        scratch_shapes=[
            *(pltpu.VMEM(r.shape, r.dtype) for r in results),
            pltpu.SemaphoreType.DMA((2, 8)),
        ],
        name="hand_over",
    )(*done)


def solution(mesh):
    placed = (
        P("dp", "mp"), P("dp", None), P(), P(), P(), P(None, "mp"), P(), P(), P(None, "mp"), P("dp", "mp"),
    )
    return jax.shard_map(
        shards, mesh=mesh, in_specs=placed, out_specs=(P("dp", "mp"),) * 4, check_vma=False,
    )
```

```python
import functools

import jax
import jax.numpy as jnp
from jax import lax
from jax.experimental import pallas as pl
from jax.experimental.pallas import tpu as pltpu
from jax.sharding import PartitionSpec as P

MESH = pl.DeviceIdType.MESH
BF, F32 = jnp.bfloat16, jnp.float32
N_DP, RING = 8, 4
ROWS = 384
SLOTS = 48
FEAT = 384
D = 6144
HEAD = 128
HEADS_DEV = 2
QKV = 3 * HEAD * HEADS_DEV
OUT = HEAD * HEADS_DEV
GRAD_ROWS = D // N_DP
HALF, QUART = ROWS // 2, ROWS // 4
EPSILON = 1e-06
SCALE = HEAD ** (-0.5)
N_SEMS = 256


def dot(a, b):
    return jnp.dot(a, b, preferred_element_type=F32)


def dot_nt(a, b):
    return lax.dot_general(a, b, (((1,), (1,)), ((), ())), preferred_element_type=F32)


def dot_tn(a, b):
    return lax.dot_general(a, b, (((0,), (0,)), ((), ())), preferred_element_type=F32)


def head_norm(values):
    centred = values - jnp.mean(values, axis=-1, keepdims=True)
    variance = jnp.mean(centred * centred, axis=-1, keepdims=True)
    inverse = lax.rsqrt(variance + EPSILON)
    return centred * inverse, inverse


def head_norm_back(incoming, normed, inverse, gain):
    scaled = incoming * gain
    return (
        scaled
        - jnp.mean(scaled, axis=-1, keepdims=True)
        - normed * jnp.mean(scaled * normed, axis=-1, keepdims=True)
    ) * inverse


def kernel(
    count_hbm, dest_hbm, offset_hbm, keep_hbm, qg_hbm, kg_hbm, patches_hbm, cot_hbm, wq_hbm, wo_hbm,
    block_hbm, pgrad_hbm, qkv_hbm, out_hbm,
    count_ref, dest_ref, offset_ref, keep_ref, qg_ref, kg_ref, patches_ref, cot_ref,
    block_ref, pgrad_ref, qkv_ref, out_ref,
    wq, wo, xf, gf, term, pj, gp, att, ga, qb, kb, probs, bias, sel_t, pack, own_x, own_g,
    og, ar, og2, ar2, rb1, rb2, pq, cq, rq, po, co, ro, ssem, rsem, lsem,
):
    dp, mp = lax.axis_index("dp"), lax.axis_index("mp")
    x, c = dp // 2, dp % 2
    y, z = mp // RING, mp % RING
    counter = [0]

    def at_mp(yy, zz):
        return (dp, (yy % RING) * RING + zz % RING)

    def at_dp(xx, cc):
        return ((xx % RING) * 2 + cc, mp)

    def along(axis, step):
        if axis == "y":
            return at_mp(y + RING + step, z)
        if axis == "z":
            return at_mp(y, z + RING + step)
        return at_dp(x + RING + step, c)

    def remote(src, dst, device):
        k = counter[0]
        counter[0] += 1
        return pltpu.make_async_remote_copy(
            src_ref=src, dst_ref=dst, send_sem=ssem.at[k], recv_sem=rsem.at[k],
            device_id=device, device_id_type=MESH,
        )

    sent = {}

    def start(copy):
        copy.start()
        sent[id(copy)] = copy

    def settle(copies):
        for copy in copies:
            sent.pop(id(copy)).wait_send()

    def column(dy, dz):
        block = ((y + dy) % RING) * RING + (z + dz) % RING
        return pl.ds(pl.multiple_of(block * FEAT, 128), FEAT)

    class Gather:
        def __init__(self, full):
            self.full = full
            self.one, self.fwd, self.two, self.fwd2 = {}, {}, {}, {}
            for h in (0, 1):
                a, b = ("y", "z") if h == 0 else ("z", "y")
                for s in (1, -1):
                    self.one[h, s] = self.copy(h, 0, 0, 0, HALF, a, s)
                    self.fwd[h, s] = self.copy(h, -s, 0, 0 if s == 1 else QUART, QUART, a, s)
                    for da in (0, 1, -1, 2):
                        self.two[h, da, s] = self.copy(h, da, 0, 0, HALF, b, s)
                        self.fwd2[h, da, s] = self.copy(h, da, -s, 0 if s == 1 else QUART, QUART, b, s)

        def copy(self, h, da, db, low, n, axis, s):
            dy, dz = (da, db) if h == 0 else (db, da)
            ref = self.full.at[pl.ds(h * HALF + low, n), column(dy + RING, dz + RING)]
            return remote(ref, ref, along(axis, s))

        def begin(self):
            for s in (1, -1):
                for h in (0, 1):
                    start(self.one[h, s])

        def second(self, da):
            for s in (1, -1):
                for h in (0, 1):
                    start(self.two[h, da, s])

        def forward(self, then=True):
            for s in (1, -1):
                for h in (0, 1):
                    self.one[h, s].wait_recv()
                    start(self.fwd[h, s])
            if then:
                self.second(1)
                self.second(-1)

        def opposite(self):
            for s in (1, -1):
                for h in (0, 1):
                    self.fwd[h, s].wait_recv()

        def forward2(self, da):
            for s in (1, -1):
                for h in (0, 1):
                    self.two[h, da, s].wait_recv()
                    start(self.fwd2[h, da, s])

        def copies(self):
            return [copy for group in (self.one, self.fwd, self.two, self.fwd2) for copy in group.values()]

        def finish(self, das=(0, 1, -1, 2)):
            for da in das:
                for s in (1, -1):
                    for h in (0, 1):
                        self.fwd2[h, da, s].wait_recv()

    class Ring:
        def __init__(self, part, box, rows, axis, chunk=None):
            half = rows // 2
            self.part, self.box, self.rows, self.half = part, box, rows, half
            self.chunk = chunk
            self.c0 = remote(part(2, 0, half), box(0, half), along(axis, 1))
            self.c1 = remote(part(2, half, half), box(half, half), along(axis, -1))
            self.c2 = remote(part(1, half, half), box(rows + half, half), along(axis, 1))
            self.c3 = remote(part(3, 0, half), box(2 * rows, half), along(axis, -1))
            self.c4 = remote(part(1, 0, half), box(rows, half), along(axis, 1))
            self.c5 = remote(part(3, half, half), box(2 * rows + half, half), along(axis, -1))

        def far(self):
            start(self.c0)
            start(self.c1)

        def near(self):
            start(self.c2)
            start(self.c3)

        def add(self, r, low, box_low):
            if self.chunk is None:
                ref = self.part(r, low, self.half)
                ref[...] = (ref[...].astype(F32) + self.box(box_low, self.half)[...].astype(F32)).astype(BF)
                return

            @pl.loop(0, self.half // self.chunk)
            def _(i):
                step = pl.multiple_of(i * self.chunk, self.chunk)
                ref = self.part(r, low + step, self.chunk)
                ref[...] = (ref[...].astype(F32) + self.box(box_low + step, self.chunk)[...].astype(F32)).astype(BF)

        def pass_on(self):
            self.c0.wait_recv()
            self.add(1, 0, 0)
            start(self.c4)
            self.c1.wait_recv()
            self.add(3, self.half, self.half)
            start(self.c5)

        def arrive(self):
            for copy in (self.c2, self.c3, self.c4, self.c5):
                copy.wait_recv()

        def total(self, low, n):
            return (
                self.part(0, low, n)[...].astype(F32)
                + self.box(self.rows + low, n)[...].astype(F32)
                + self.box(2 * self.rows + low, n)[...].astype(F32)
            )

    class Scatter:
        def __init__(self, terms, boxes):
            self.first, self.last = {}, {}
            for h in (0, 1):
                a, b = ("z", "y") if h == 0 else ("y", "z")

                def piece(r1, r2, low, n, h=h):
                    slot = r2 * RING + r1 if h == 0 else r1 * RING + r2
                    return terms.at[pl.ds(h * HALF + low, n), pl.ds(slot * FEAT, FEAT)]

                for r2 in range(RING):
                    self.first[h, r2] = Ring(
                        lambda r, low, n, r2=r2, piece=piece: piece(r, r2, low, n),
                        lambda low, n, h=h, r2=r2: boxes.at[h, r2, pl.ds(low, n)],
                        HALF, a,
                    )
                self.last[h] = Ring(
                    lambda r, low, n, piece=piece: piece(0, r, low, n),
                    lambda low, n, h=h: boxes.at[h, RING, pl.ds(low, n)],
                    HALF, b,
                )

        def send(self, r2):
            for h in (0, 1):
                self.first[h, r2].far()
            for h in (0, 1):
                self.first[h, r2].near()

        def pass_on(self, r2):
            for h in (0, 1):
                self.first[h, r2].pass_on()

        def collect(self, r2):
            for h in (0, 1):
                ring = self.first[h, r2]
                ring.arrive()
                ring.part(0, 0, HALF)[...] = ring.total(0, HALF).astype(BF)
                if r2 == 2:
                    self.last[h].far()
            if r2 == 3:
                for h in (0, 1):
                    self.last[h].near()

        def last_pass(self):
            for h in (0, 1):
                self.last[h].pass_on()

        def result(self, h):
            self.last[h].arrive()
            return self.last[h].total(0, HALF)

    class WeightGrad:
        def __init__(self, rows, cols, width, mine, theirs, boxes, slots, result):
            self.rows, self.cols, self.mine, self.theirs, self.result = rows, cols, mine, theirs, result
            self.slots = slots
            self.swap = {
                dx: remote(mine.at[i % slots], theirs.at[dx], at_dp(x, 1 - c)) for i, dx in enumerate((2, 1, 3, 0))
            }
            self.ring = Ring(
                lambda r, low, n: theirs.at[r, pl.ds(low, n)], lambda low, n: boxes.at[pl.ds(low, n)],
                GRAD_ROWS, "x", chunk=64,
            )
            self.order = []

        def tile(self, dx, core):
            block = ((x + dx) % RING) * 2 + core
            left = self.rows[:, pl.ds(pl.multiple_of(block * GRAD_ROWS, 128), GRAD_ROWS)]
            return dot_tn(left, self.cols[...])

        def send(self, dx):
            i = len(self.order)
            if i >= self.slots:
                self.swap[self.order[i - self.slots]].wait_send()
            self.order.append(dx)
            self.mine[i % self.slots] = self.tile(dx, 1 - c).astype(BF)
            self.swap[dx].start()

        def add(self, dx):
            self.swap[dx].wait_recv()
            value = self.tile(dx, c) + self.theirs[dx].astype(F32)
            if dx == 0:
                self.result[...] = value
            else:
                self.theirs[dx] = value.astype(BF)

            if dx == 2:
                self.ring.far()
            if dx == 3:
                self.ring.near()

        def gain(self, low, box_low, n=GRAD_ROWS // 2, step=64):
            @pl.loop(0, n // step)
            def _(i):
                more = pl.multiple_of(i * step, step)
                at = pl.ds(low + more, step)
                self.result[at, :] += self.ring.box(box_low + more, step)[...].astype(F32)

        def begin_finish(self):
            half = GRAD_ROWS // 2
            self.ring.c2.wait_recv()
            self.gain(half, GRAD_ROWS + half)
            self.ring.c3.wait_recv()
            self.gain(0, 2 * GRAD_ROWS)

        def finish(self, target, sems):
            half = GRAD_ROWS // 2
            for copy, low, box_low, sem in (
                (self.ring.c4, 0, GRAD_ROWS, sems[0]), (self.ring.c5, half, 2 * GRAD_ROWS + half, sems[1]),
            ):
                copy.wait_recv()
                self.gain(low, box_low)
                at = pl.ds(low, half)
                saved(pltpu.make_async_copy(self.result.at[at], target.at[at], lsem.at[sem]))

        def close(self):
            for dx in self.order[-self.slots:]:
                self.swap[dx].wait_send()

    loads = [
        pltpu.make_async_copy(source, target, lsem.at[6 + i])
        for i, (source, target) in enumerate((
            (count_hbm, count_ref), (dest_hbm, dest_ref), (offset_hbm, offset_ref), (keep_hbm, keep_ref),
            (cot_hbm, cot_ref), (patches_hbm, patches_ref), (qg_hbm, qg_ref), (kg_hbm, kg_ref),
        ))
    ]
    for copy in loads:
        copy.start()
    load_q = pltpu.make_async_copy(wq_hbm, wq, lsem.at[0])
    load_o = pltpu.make_async_copy(wo_hbm, wo, lsem.at[1])

    barrier = pltpu.get_barrier_semaphore()
    for axis in ("y", "z"):
        for s in (1, -1):
            pl.semaphore_signal(barrier, inc=1, device_id=along(axis, s), device_id_type=MESH)
    for o in range(1, N_DP):
        pl.semaphore_signal(barrier, inc=1, device_id=((dp + o) % N_DP, mp), device_id_type=MESH)

    load_q.start()
    load_o.start()

    def saved(copy):
        copy.start()
        saves.append(copy)

    saves = []
    for copy in loads:
        copy.wait()
    lane = lax.broadcasted_iota(jnp.int32, (1, ROWS), 1)
    part = (lane * 1366) >> 16
    slot = lane - part * SLOTS
    off = jnp.full((1, ROWS), -1, jnp.int32)
    total_rows = 0
    for t in range(N_DP):
        base, here_count = 0, 0
        for k in range(N_DP):
            mine = dest_ref[t * N_DP + k] == dp
            base += jnp.where(mine, offset_ref[t * N_DP + k], 0)
            here_count += jnp.where(mine, count_ref[t * N_DP + k], 0)
        off = jnp.where((part == t) & (slot < here_count), base + slot, off)
        total_rows += here_count
    spread_row = lax.broadcasted_iota(jnp.int32, (SLOTS, ROWS), 0)
    spread = (spread_row == slot).astype(F32).astype(BF)
    kept = dot(keep_ref[...].astype(F32).astype(BF), spread).astype(jnp.int32)
    src = jnp.full((1, ROWS), -1, jnp.int32)
    for k in range(N_DP):
        goes = (part == dest_ref[dp * N_DP + k]) & (slot < count_ref[dp * N_DP + k])
        src = jnp.where(goes, kept[k:k + 1, :] + k * SLOTS, src)
    row_id = lax.broadcasted_iota(jnp.int32, (ROWS, ROWS), 0)
    col_id = lax.broadcasted_iota(jnp.int32, (ROWS, ROWS), 1)
    row_live = row_id < total_rows
    col_live = col_id < total_rows
    own_g[...] = jnp.where(row_live, cot_ref[...].astype(F32), 0.0).astype(BF)
    gf[:, column(0, 0)] = own_g[...]
    sel_t[...] = (row_id == src).astype(F32).astype(BF)
    og[...] = dot_tn(sel_t[...], patches_ref[...]).astype(BF)

    gather_g, gather_x = Gather(gf), Gather(xf)
    swap_x = [
        remote(og.at[pl.ds(pl.multiple_of(((dp + o) % N_DP) * SLOTS, SLOTS), SLOTS)],
               ar.at[pl.ds(pl.multiple_of(dp * SLOTS, SLOTS), SLOTS)], ((dp + o) % N_DP, mp))
        for o in range(1, N_DP)
    ]
    swap_g = [
        remote(og2.at[pl.ds(pl.multiple_of(((dp + o) % N_DP) * SLOTS, SLOTS), SLOTS)],
               ar2.at[pl.ds(pl.multiple_of(dp * SLOTS, SLOTS), SLOTS)], ((dp + o) % N_DP, mp))
        for o in range(1, N_DP)
    ]
    scatter_p, scatter_b = Scatter(term, rb1), Scatter(gf, rb2)
    grad_q = WeightGrad(xf, gp, QKV, pq, cq, rq, 2, qkv_ref)
    grad_o = WeightGrad(gf, att, OUT, po, co, ro, 4, out_ref)
    assert counter[0] <= N_SEMS

    pl.semaphore_wait(barrier, 4 + N_DP - 1)
    for copy in swap_x:
        start(copy)
    gather_g.begin()
    gather_g.second(0)
    here = pl.ds(pl.multiple_of(dp * SLOTS, SLOTS), SLOTS)
    ar[here, :] = og[here, :]
    pack[...] = (row_id == off).astype(F32).astype(BF)
    for copy in swap_x:
        copy.wait_recv()
    own_x[...] = dot(pack[...], ar[...]).astype(BF)
    xf[:, column(0, 0)] = own_x[...]
    gather_x.begin()
    gather_x.second(0)
    gather_g.forward(then=False)
    gather_x.forward()
    gather_g.opposite()
    gather_x.opposite()
    gather_x.second(2)
    same = ((row_id * 1366) >> 16) == ((col_id * 1366) >> 16)
    image = dot(pack[...], same.astype(F32).astype(BF)).astype(BF)
    both = dot_nt(image, pack[...]) > 0.5
    bias[...] = jnp.where(both | (jnp.logical_not(row_live) & jnp.logical_not(col_live)), 0.0, -jnp.inf)
    for da in (0, 1, -1):
        gather_x.forward2(da)
    gather_g.forward2(0)
    gather_x.forward2(2)
    for da in (1, -1, 2):
        gather_g.second(da)
    gather_x.finish()
    load_q.wait()

    def project(n):
        at = slice(n * 256, (n + 1) * 256)
        pj[:, at] = dot(xf[...], wq[:, at]).astype(BF)

    def head_forward(h):
        base = h * 3 * HEAD
        query, _ = head_norm(pj[:, base:base + HEAD].astype(F32))
        keys, _ = head_norm(pj[:, base + HEAD:base + 2 * HEAD].astype(F32))
        qb[h] = (query * qg_ref[...]).astype(BF)
        kb[h] = (keys * kg_ref[...]).astype(BF)
        scores = dot_nt(qb[h], kb[h]) * SCALE + bias[...]
        exponent = jnp.exp(scores - jnp.max(scores, axis=-1, keepdims=True))
        prob = exponent / jnp.sum(exponent, axis=-1, keepdims=True)
        probs[h] = prob
        att[:, h * HEAD:(h + 1) * HEAD] = dot(prob.astype(BF), pj[:, base + 2 * HEAD:base + 3 * HEAD]).astype(BF)

    def head_backward(h):
        base = h * 3 * HEAD
        value = pj[:, base + 2 * HEAD:base + 3 * HEAD]
        incoming = ga[:, h * HEAD:(h + 1) * HEAD]
        prob = probs[h]
        gp[:, base + 2 * HEAD:base + 3 * HEAD] = dot_tn(prob.astype(BF), incoming).astype(BF)
        grad_probs = dot_nt(incoming, value)
        grad_scores = (prob * (grad_probs - jnp.sum(prob * grad_probs, axis=-1, keepdims=True)) * SCALE).astype(BF)
        query, query_inv = head_norm(pj[:, base:base + HEAD].astype(F32))
        keys, key_inv = head_norm(pj[:, base + HEAD:base + 2 * HEAD].astype(F32))
        grad_qn = dot(grad_scores, kb[h])
        grad_kn = dot_tn(grad_scores, qb[h])
        gp[:, base:base + HEAD] = head_norm_back(grad_qn, query, query_inv, qg_ref[...]).astype(BF)
        gp[:, base + HEAD:base + 2 * HEAD] = head_norm_back(grad_kn, keys, key_inv, kg_ref[...]).astype(BF)

    def make_terms(group, left, weights, terms):
        def some(places):
            blocks = []
            for dy, dz in places:
                block = ((y + dy) % RING) * RING + (z + dz) % RING
                blocks.append(weights[pl.ds(pl.multiple_of(block * FEAT, 128), FEAT), :])
            value = dot_nt(left[...], jnp.concatenate(blocks, axis=0)).astype(BF)
            for i, (dy, dz) in enumerate(places):
                terms[:, pl.ds((dy * RING + dz) * FEAT, FEAT)] = value[:, i * FEAT:(i + 1) * FEAT]

        if group == 0:
            some([(2, 1), (2, 2), (2, 3)])
            some([(1, 2), (3, 2)])
        elif group == 1:
            some([(1, 1), (1, 3)])
            some([(3, 1), (3, 3)])
        else:
            some([(0, 1), (0, 2), (0, 3)])
            some([(1, 0), (2, 0), (3, 0), (0, 0)])

    project(0)
    project(1)
    gather_g.forward2(1)
    project(2)
    head_forward(0)
    gather_g.forward2(-1)
    head_forward(1)
    load_o.wait()
    make_terms(0, att, wo, term)
    gather_g.forward2(2)
    scatter_p.send(2)
    make_terms(1, att, wo, term)
    scatter_p.send(1)
    scatter_p.send(3)
    make_terms(2, att, wo, term)
    scatter_p.send(0)
    gather_g.finish()

    def grad_attended():
        ga[...] = dot(gf[...], wo[...]).astype(BF)

    grad_o.send(2)
    grad_o.send(1)
    grad_o.send(3)
    grad_attended()
    grad_o.add(2)
    grad_o.add(1)
    grad_o.add(3)
    scatter_p.pass_on(2)
    head_backward(0)
    head_backward(1)
    grad_q.send(2)
    grad_q.send(1)
    scatter_p.pass_on(1)
    grad_q.add(2)
    grad_q.send(3)
    grad_o.ring.pass_on()
    grad_q.add(1)
    scatter_p.pass_on(3)
    grad_q.add(3)
    scatter_p.pass_on(0)
    grad_o.send(0)
    scatter_p.collect(2)
    grad_o.add(0)
    settle(gather_g.copies())
    make_terms(0, gp, wq, gf)
    scatter_b.send(2)
    scatter_p.collect(1)
    scatter_p.collect(3)
    make_terms(1, gp, wq, gf)
    scatter_b.send(1)
    scatter_b.send(3)
    scatter_p.last_pass()
    make_terms(2, gp, wq, gf)
    scatter_b.send(0)
    scatter_p.collect(0)
    scatter_b.pass_on(2)
    for h in (0, 1):
        rows = pl.ds(h * HALF, HALF)
        live = lax.broadcasted_iota(jnp.int32, (HALF, FEAT), 0) + h * HALF < total_rows
        value = own_x[rows, :].astype(F32) + scatter_p.result(h)
        block_ref[rows, :] = jnp.where(live, value, 0.0).astype(BF)
    saved(pltpu.make_async_copy(block_ref, block_hbm, lsem.at[2]))
    grad_q.ring.pass_on()
    scatter_b.pass_on(1)
    grad_q.send(0)
    scatter_b.pass_on(3)
    grad_o.begin_finish()
    grad_o.finish(out_hbm, (3, 14))
    scatter_b.pass_on(0)
    scatter_b.collect(2)
    grad_q.add(0)
    scatter_b.collect(1)
    scatter_b.collect(3)
    scatter_b.last_pass()
    scatter_b.collect(0)
    for h in (0, 1):
        rows = pl.ds(h * HALF, HALF)
        own_g[rows, :] = (own_g[rows, :].astype(F32) + scatter_b.result(h)).astype(BF)
    og2[...] = dot_tn(pack[...], own_g[...]).astype(BF)
    for copy in swap_g:
        start(copy)
    ar2[here, :] = og2[here, :]
    grad_q.begin_finish()
    for copy in swap_g:
        copy.wait_recv()
    pgrad_ref[...] = dot(sel_t[...], ar2[...]).astype(BF)
    saved(pltpu.make_async_copy(pgrad_ref, pgrad_hbm, lsem.at[5]))
    grad_q.finish(qkv_hbm, (4, 15))
    grad_q.close()
    grad_o.close()
    settle(list(sent.values()))
    for copy in saves:
        copy.wait()


def hand_over(*refs):
    inputs, outputs, held, sems = refs[:4], refs[4:8], refs[8:12], refs[12]
    pairs = []
    for source, target, stage in zip(inputs, outputs, held):
        pieces = max(1, source.shape[0] * source.shape[1] // (192 * 768))
        step = source.shape[0] // pieces
        for p in range(pieces):
            at = pl.ds(p * step, step)
            k = len(pairs)
            pairs.append((
                pltpu.make_async_copy(source.at[at], stage.at[at], sems.at[0, k]),
                pltpu.make_async_copy(stage.at[at], target.at[at], sems.at[1, k]),
            ))
    for fetch, _ in pairs:
        fetch.start()
    for fetch, store in pairs:
        fetch.wait()
        store.start()
    for _, store in pairs:
        store.wait()


def shards(
    patches, keep_index, keep_count, pack_dest, pack_offset, w_qkv, q_gain, k_gain, w_out, cotangent
):
    hbm = pl.BlockSpec(memory_space=pltpu.HBM)
    results = (
        jax.ShapeDtypeStruct((ROWS, FEAT), BF),
        jax.ShapeDtypeStruct((ROWS, FEAT), BF),
        jax.ShapeDtypeStruct((GRAD_ROWS, QKV), F32),
        jax.ShapeDtypeStruct((GRAD_ROWS, OUT), F32),
    )
    done = pl.pallas_call(
        kernel,
        out_shape=results,
        in_specs=[hbm] * 10,
        out_specs=(hbm,) * 4,
        scratch_shapes=[
            pltpu.SMEM((N_DP * N_DP,), jnp.int32),
            pltpu.SMEM((N_DP * N_DP,), jnp.int32),
            pltpu.SMEM((N_DP * N_DP,), jnp.int32),
            pltpu.VMEM((N_DP, SLOTS), jnp.int32),
            pltpu.VMEM((1, HEAD), F32),
            pltpu.VMEM((1, HEAD), F32),
            pltpu.VMEM((ROWS, FEAT), BF),
            pltpu.VMEM((ROWS, FEAT), BF),
            *(pltpu.VMEM(r.shape, r.dtype) for r in results),
            pltpu.VMEM((D, QKV), BF),
            pltpu.VMEM((D, OUT), BF),
            pltpu.VMEM((ROWS, D), BF),
            pltpu.VMEM((ROWS, D), BF),
            pltpu.VMEM((ROWS, D), BF),
            pltpu.VMEM((ROWS, QKV), BF),
            pltpu.VMEM((ROWS, QKV), BF),
            pltpu.VMEM((ROWS, OUT), BF),
            pltpu.VMEM((ROWS, OUT), BF),
            pltpu.VMEM((HEADS_DEV, ROWS, HEAD), BF),
            pltpu.VMEM((HEADS_DEV, ROWS, HEAD), BF),
            pltpu.VMEM((HEADS_DEV, ROWS, ROWS), F32),
            pltpu.VMEM((ROWS, ROWS), F32),
            pltpu.VMEM((ROWS, ROWS), BF),
            pltpu.VMEM((ROWS, ROWS), BF),
            pltpu.VMEM((ROWS, FEAT), BF),
            pltpu.VMEM((ROWS, FEAT), BF),
            pltpu.VMEM((ROWS, FEAT), BF),
            pltpu.VMEM((ROWS, FEAT), BF),
            pltpu.VMEM((ROWS, FEAT), BF),
            pltpu.VMEM((ROWS, FEAT), BF),
            pltpu.VMEM((2, RING + 1, 3 * HALF, FEAT), BF),
            pltpu.VMEM((2, RING + 1, 3 * HALF, FEAT), BF),
            pltpu.VMEM((2, GRAD_ROWS, QKV), BF),
            pltpu.VMEM((RING, GRAD_ROWS, QKV), BF),
            pltpu.VMEM((3 * GRAD_ROWS, QKV), BF),
            pltpu.VMEM((4, GRAD_ROWS, OUT), BF),
            pltpu.VMEM((RING, GRAD_ROWS, OUT), BF),
            pltpu.VMEM((3 * GRAD_ROWS, OUT), BF),
            pltpu.SemaphoreType.DMA((N_SEMS,)),
            pltpu.SemaphoreType.DMA((N_SEMS,)),
            pltpu.SemaphoreType.DMA((16,)),
        ],
        compiler_params=pltpu.CompilerParams(
            collective_id=0, has_side_effects=True, vmem_limit_bytes=63 << 20
        ),
        cost_estimate=pl.CostEstimate(flops=15_000_000_000, bytes_accessed=20_000_000, transcendentals=300_000),
        name="block",
    )(
        keep_count, pack_dest, pack_offset, keep_index, q_gain.reshape(1, HEAD), k_gain.reshape(1, HEAD),
        patches, cotangent, w_qkv, w_out,
    )
    return pl.pallas_call(
        hand_over,
        out_shape=results,
        in_specs=[hbm] * 4,
        out_specs=(hbm,) * 4,
        scratch_shapes=[
            *(pltpu.VMEM(r.shape, r.dtype) for r in results),
            pltpu.SemaphoreType.DMA((2, 8)),
        ],
        name="hand_over",
    )(*done)


def solution(mesh):
    placed = (
        P("dp", "mp"), P("dp", None), P(), P(), P(), P(None, "mp"), P(), P(), P(None, "mp"), P("dp", "mp"),
    )
    return jax.shard_map(
        shards, mesh=mesh, in_specs=placed, out_specs=(P("dp", "mp"),) * 4, check_vma=False,
    )
```

```python
import functools

import jax
import jax.numpy as jnp
from jax import lax
from jax.experimental import pallas as pl
from jax.experimental.pallas import tpu as pltpu
from jax.sharding import PartitionSpec as P

MESH = pl.DeviceIdType.MESH
BF, F32 = jnp.bfloat16, jnp.float32
N_DP, RING = 8, 4
ROWS = 384
SLOTS = 48
FEAT = 384
D = 6144
HEAD = 128
HEADS_DEV = 2
QKV = 3 * HEAD * HEADS_DEV
OUT = HEAD * HEADS_DEV
GRAD_ROWS = D // N_DP
HALF, QUART = ROWS // 2, ROWS // 4
EPSILON = 1e-06
SCALE = HEAD ** (-0.5)
N_SEMS = 256


def dot(a, b):
    return jnp.dot(a, b, preferred_element_type=F32)


def dot_nt(a, b):
    return lax.dot_general(a, b, (((1,), (1,)), ((), ())), preferred_element_type=F32)


def dot_tn(a, b):
    return lax.dot_general(a, b, (((0,), (0,)), ((), ())), preferred_element_type=F32)


def head_norm(values):
    centred = values - jnp.mean(values, axis=-1, keepdims=True)
    variance = jnp.mean(centred * centred, axis=-1, keepdims=True)
    inverse = lax.rsqrt(variance + EPSILON)
    return centred * inverse, inverse


def head_norm_back(incoming, normed, inverse, gain):
    scaled = incoming * gain
    return (
        scaled
        - jnp.mean(scaled, axis=-1, keepdims=True)
        - normed * jnp.mean(scaled * normed, axis=-1, keepdims=True)
    ) * inverse


def kernel(
    count_hbm, dest_hbm, offset_hbm, keep_hbm, qg_hbm, kg_hbm, patches_hbm, cot_hbm, wq_hbm, wo_hbm,
    block_hbm, pgrad_hbm, qkv_hbm, out_hbm,
    count_ref, dest_ref, offset_ref, keep_ref, qg_ref, kg_ref, patches_ref, cot_ref,
    block_ref, pgrad_ref, qkv_ref, out_ref,
    wq, wo, xf, gf, term, pj, gp, att, ga, qb, kb, probs, bias, sel_t, pack, own_x, own_g,
    og, ar, og2, ar2, rb1, rb2, pq, cq, rq, po, co, ro, ssem, rsem, lsem,
):
    dp, mp = lax.axis_index("dp"), lax.axis_index("mp")
    x, c = dp // 2, dp % 2
    y, z = mp // RING, mp % RING
    counter = [0]

    def at_mp(yy, zz):
        return (dp, (yy % RING) * RING + zz % RING)

    def at_dp(xx, cc):
        return ((xx % RING) * 2 + cc, mp)

    def along(axis, step):
        if axis == "y":
            return at_mp(y + RING + step, z)
        if axis == "z":
            return at_mp(y, z + RING + step)
        return at_dp(x + RING + step, c)

    def remote(src, dst, device):
        k = counter[0]
        counter[0] += 1
        return pltpu.make_async_remote_copy(
            src_ref=src, dst_ref=dst, send_sem=ssem.at[k], recv_sem=rsem.at[k],
            device_id=device, device_id_type=MESH,
        )

    sent = {}

    def start(copy):
        copy.start()
        sent[id(copy)] = copy

    def settle(copies):
        for copy in copies:
            sent.pop(id(copy)).wait_send()

    def column(dy, dz):
        block = ((y + dy) % RING) * RING + (z + dz) % RING
        return pl.ds(pl.multiple_of(block * FEAT, 128), FEAT)

    class Gather:
        def __init__(self, full):
            self.full = full
            self.one, self.fwd, self.two, self.fwd2 = {}, {}, {}, {}
            for h in (0, 1):
                a, b = ("y", "z") if h == 0 else ("z", "y")
                for s in (1, -1):
                    self.one[h, s] = self.copy(h, 0, 0, 0, HALF, a, s)
                    self.fwd[h, s] = self.copy(h, -s, 0, 0 if s == 1 else QUART, QUART, a, s)
                    for da in (0, 1, -1, 2):
                        self.two[h, da, s] = self.copy(h, da, 0, 0, HALF, b, s)
                        self.fwd2[h, da, s] = self.copy(h, da, -s, 0 if s == 1 else QUART, QUART, b, s)

        def copy(self, h, da, db, low, n, axis, s):
            dy, dz = (da, db) if h == 0 else (db, da)
            ref = self.full.at[pl.ds(h * HALF + low, n), column(dy + RING, dz + RING)]
            return remote(ref, ref, along(axis, s))

        def begin(self):
            for s in (1, -1):
                for h in (0, 1):
                    start(self.one[h, s])

        def second(self, da):
            for s in (1, -1):
                for h in (0, 1):
                    start(self.two[h, da, s])

        def forward(self, then=True):
            for s in (1, -1):
                for h in (0, 1):
                    self.one[h, s].wait_recv()
                    start(self.fwd[h, s])
            if then:
                self.second(1)
                self.second(-1)

        def opposite(self):
            for s in (1, -1):
                for h in (0, 1):
                    self.fwd[h, s].wait_recv()

        def forward2(self, da):
            for s in (1, -1):
                for h in (0, 1):
                    self.two[h, da, s].wait_recv()
                    start(self.fwd2[h, da, s])

        def copies(self):
            return [copy for group in (self.one, self.fwd, self.two, self.fwd2) for copy in group.values()]

        def finish(self, das=(0, 1, -1, 2)):
            for da in das:
                for s in (1, -1):
                    for h in (0, 1):
                        self.fwd2[h, da, s].wait_recv()

    class Ring:
        def __init__(self, part, box, rows, axis, chunk=None):
            half = rows // 2
            self.part, self.box, self.rows, self.half = part, box, rows, half
            self.chunk = chunk
            self.c0 = remote(part(2, 0, half), box(0, half), along(axis, 1))
            self.c1 = remote(part(2, half, half), box(half, half), along(axis, -1))
            self.c2 = remote(part(1, half, half), box(rows + half, half), along(axis, 1))
            self.c3 = remote(part(3, 0, half), box(2 * rows, half), along(axis, -1))
            self.c4 = remote(part(1, 0, half), box(rows, half), along(axis, 1))
            self.c5 = remote(part(3, half, half), box(2 * rows + half, half), along(axis, -1))

        def far(self):
            start(self.c0)
            start(self.c1)

        def near(self):
            start(self.c2)
            start(self.c3)

        def add(self, r, low, box_low):
            if self.chunk is None:
                ref = self.part(r, low, self.half)
                ref[...] = (ref[...].astype(F32) + self.box(box_low, self.half)[...].astype(F32)).astype(BF)
                return

            @pl.loop(0, self.half // self.chunk)
            def _(i):
                step = pl.multiple_of(i * self.chunk, self.chunk)
                ref = self.part(r, low + step, self.chunk)
                ref[...] = (ref[...].astype(F32) + self.box(box_low + step, self.chunk)[...].astype(F32)).astype(BF)

        def pass_on(self):
            self.c0.wait_recv()
            self.add(1, 0, 0)
            start(self.c4)
            self.c1.wait_recv()
            self.add(3, self.half, self.half)
            start(self.c5)

        def arrive(self):
            for copy in (self.c2, self.c3, self.c4, self.c5):
                copy.wait_recv()

        def total(self, low, n):
            return (
                self.part(0, low, n)[...].astype(F32)
                + self.box(self.rows + low, n)[...].astype(F32)
                + self.box(2 * self.rows + low, n)[...].astype(F32)
            )

    class Scatter:
        def __init__(self, terms, boxes):
            self.first, self.last = {}, {}
            for h in (0, 1):
                a, b = ("z", "y") if h == 0 else ("y", "z")

                def piece(r1, r2, low, n, h=h):
                    slot = r2 * RING + r1 if h == 0 else r1 * RING + r2
                    return terms.at[pl.ds(h * HALF + low, n), pl.ds(slot * FEAT, FEAT)]

                for r2 in range(RING):
                    self.first[h, r2] = Ring(
                        lambda r, low, n, r2=r2, piece=piece: piece(r, r2, low, n),
                        lambda low, n, h=h, r2=r2: boxes.at[h, r2, pl.ds(low, n)],
                        HALF, a,
                    )
                self.last[h] = Ring(
                    lambda r, low, n, piece=piece: piece(0, r, low, n),
                    lambda low, n, h=h: boxes.at[h, RING, pl.ds(low, n)],
                    HALF, b,
                )

        def send(self, r2):
            for h in (0, 1):
                self.first[h, r2].far()
            for h in (0, 1):
                self.first[h, r2].near()

        def pass_on(self, r2):
            for h in (0, 1):
                self.first[h, r2].pass_on()

        def collect(self, r2):
            for h in (0, 1):
                ring = self.first[h, r2]
                ring.arrive()
                ring.part(0, 0, HALF)[...] = ring.total(0, HALF).astype(BF)
                if r2 == 2:
                    self.last[h].far()
            if r2 == 3:
                for h in (0, 1):
                    self.last[h].near()

        def last_pass(self):
            for h in (0, 1):
                self.last[h].pass_on()

        def result(self, h):
            self.last[h].arrive()
            return self.last[h].total(0, HALF)

    class WeightGrad:
        def __init__(self, rows, cols, width, mine, theirs, boxes, slots, result):
            self.rows, self.cols, self.mine, self.theirs, self.result = rows, cols, mine, theirs, result
            self.slots = slots
            self.swap = {
                dx: remote(mine.at[i % slots], theirs.at[dx], at_dp(x, 1 - c)) for i, dx in enumerate((2, 1, 3, 0))
            }
            self.ring = Ring(
                lambda r, low, n: theirs.at[r, pl.ds(low, n)], lambda low, n: boxes.at[pl.ds(low, n)],
                GRAD_ROWS, "x", chunk=64,
            )
            self.order = []

        def tile(self, dx, core):
            block = ((x + dx) % RING) * 2 + core
            left = self.rows[:, pl.ds(pl.multiple_of(block * GRAD_ROWS, 128), GRAD_ROWS)]
            return dot_tn(left, self.cols[...])

        def send(self, dx):
            i = len(self.order)
            if i >= self.slots:
                self.swap[self.order[i - self.slots]].wait_send()
            self.order.append(dx)
            self.mine[i % self.slots] = self.tile(dx, 1 - c).astype(BF)
            self.swap[dx].start()

        def add(self, dx):
            self.swap[dx].wait_recv()
            value = self.tile(dx, c) + self.theirs[dx].astype(F32)
            if dx == 0:
                self.result[...] = value
            else:
                self.theirs[dx] = value.astype(BF)

            if dx == 2:
                self.ring.far()
            if dx == 3:
                self.ring.near()

        def gain(self, low, box_low, n=GRAD_ROWS // 2, step=64):
            @pl.loop(0, n // step)
            def _(i):
                more = pl.multiple_of(i * step, step)
                at = pl.ds(low + more, step)
                self.result[at, :] += self.ring.box(box_low + more, step)[...].astype(F32)

        def begin_finish(self):
            half = GRAD_ROWS // 2
            self.ring.c2.wait_recv()
            self.gain(half, GRAD_ROWS + half)
            self.ring.c3.wait_recv()
            self.gain(0, 2 * GRAD_ROWS)

        def finish(self, target, sems):
            half = GRAD_ROWS // 2
            for copy, low, box_low, sem in (
                (self.ring.c4, 0, GRAD_ROWS, sems[0]), (self.ring.c5, half, 2 * GRAD_ROWS + half, sems[1]),
            ):
                copy.wait_recv()
                self.gain(low, box_low)
                at = pl.ds(low, half)
                saved(pltpu.make_async_copy(self.result.at[at], target.at[at], lsem.at[sem]))

        def close(self):
            for dx in self.order[-self.slots:]:
                self.swap[dx].wait_send()

    loads = [
        pltpu.make_async_copy(source, target, lsem.at[6 + i])
        for i, (source, target) in enumerate((
            (count_hbm, count_ref), (dest_hbm, dest_ref), (offset_hbm, offset_ref), (keep_hbm, keep_ref),
            (cot_hbm, cot_ref), (patches_hbm, patches_ref), (qg_hbm, qg_ref), (kg_hbm, kg_ref),
        ))
    ]
    for copy in loads:
        copy.start()
    load_q = pltpu.make_async_copy(wq_hbm, wq, lsem.at[0])
    load_o = pltpu.make_async_copy(wo_hbm, wo, lsem.at[1])

    barrier = pltpu.get_barrier_semaphore()
    for axis in ("y", "z"):
        for s in (1, -1):
            pl.semaphore_signal(barrier, inc=1, device_id=along(axis, s), device_id_type=MESH)
    for o in range(1, N_DP):
        pl.semaphore_signal(barrier, inc=1, device_id=((dp + o) % N_DP, mp), device_id_type=MESH)

    load_q.start()
    load_o.start()

    def saved(copy):
        copy.start()
        saves.append(copy)

    saves = []
    for copy in loads:
        copy.wait()
    lane = lax.broadcasted_iota(jnp.int32, (1, ROWS), 1)
    part = (lane * 1366) >> 16
    slot = lane - part * SLOTS
    off = jnp.full((1, ROWS), -1, jnp.int32)
    total_rows = 0
    for t in range(N_DP):
        base, here_count = 0, 0
        for k in range(N_DP):
            mine = dest_ref[t * N_DP + k] == dp
            base += jnp.where(mine, offset_ref[t * N_DP + k], 0)
            here_count += jnp.where(mine, count_ref[t * N_DP + k], 0)
        off = jnp.where((part == t) & (slot < here_count), base + slot, off)
        total_rows += here_count
    spread_row = lax.broadcasted_iota(jnp.int32, (SLOTS, ROWS), 0)
    spread = (spread_row == slot).astype(F32).astype(BF)
    kept = dot(keep_ref[...].astype(F32).astype(BF), spread).astype(jnp.int32)
    src = jnp.full((1, ROWS), -1, jnp.int32)
    for k in range(N_DP):
        goes = (part == dest_ref[dp * N_DP + k]) & (slot < count_ref[dp * N_DP + k])
        src = jnp.where(goes, kept[k:k + 1, :] + k * SLOTS, src)
    row_id = lax.broadcasted_iota(jnp.int32, (ROWS, ROWS), 0)
    col_id = lax.broadcasted_iota(jnp.int32, (ROWS, ROWS), 1)
    row_live = row_id < total_rows
    col_live = col_id < total_rows
    own_g[...] = jnp.where(row_live, cot_ref[...].astype(F32), 0.0).astype(BF)
    gf[:, column(0, 0)] = own_g[...]
    sel_t[...] = (row_id == src).astype(F32).astype(BF)
    og[...] = dot_tn(sel_t[...], patches_ref[...]).astype(BF)

    gather_g, gather_x = Gather(gf), Gather(xf)
    swap_x = [
        remote(og.at[pl.ds(pl.multiple_of(((dp + o) % N_DP) * SLOTS, SLOTS), SLOTS)],
               ar.at[pl.ds(pl.multiple_of(dp * SLOTS, SLOTS), SLOTS)], ((dp + o) % N_DP, mp))
        for o in range(1, N_DP)
    ]
    swap_g = [
        remote(og2.at[pl.ds(pl.multiple_of(((dp + o) % N_DP) * SLOTS, SLOTS), SLOTS)],
               ar2.at[pl.ds(pl.multiple_of(dp * SLOTS, SLOTS), SLOTS)], ((dp + o) % N_DP, mp))
        for o in range(1, N_DP)
    ]
    scatter_p, scatter_b = Scatter(term, rb1), Scatter(gf, rb2)
    grad_q = WeightGrad(xf, gp, QKV, pq, cq, rq, 2, qkv_ref)
    grad_o = WeightGrad(gf, att, OUT, po, co, ro, 4, out_ref)
    assert counter[0] <= N_SEMS

    pl.semaphore_wait(barrier, 4 + N_DP - 1)
    for copy in swap_x:
        start(copy)
    gather_g.begin()
    gather_g.second(0)
    here = pl.ds(pl.multiple_of(dp * SLOTS, SLOTS), SLOTS)
    ar[here, :] = og[here, :]
    pack[...] = (row_id == off).astype(F32).astype(BF)
    for copy in swap_x:
        copy.wait_recv()
    own_x[...] = dot(pack[...], ar[...]).astype(BF)
    xf[:, column(0, 0)] = own_x[...]
    gather_x.begin()
    gather_x.second(0)
    gather_g.forward(then=False)
    gather_x.forward()
    gather_g.opposite()
    gather_x.opposite()
    gather_x.second(2)
    same = ((row_id * 1366) >> 16) == ((col_id * 1366) >> 16)
    image = dot(pack[...], same.astype(F32).astype(BF)).astype(BF)
    both = dot_nt(image, pack[...]) > 0.5
    bias[...] = jnp.where(both | (jnp.logical_not(row_live) & jnp.logical_not(col_live)), 0.0, -jnp.inf)
    for da in (0, 1, -1):
        gather_x.forward2(da)
    gather_g.forward2(0)
    gather_x.forward2(2)
    for da in (1, -1, 2):
        gather_g.second(da)
    gather_x.finish()
    load_q.wait()

    def project(n):
        at = slice(n * 256, (n + 1) * 256)
        pj[:, at] = dot(xf[...], wq[:, at]).astype(BF)

    def head_forward(h):
        base = h * 3 * HEAD
        query, _ = head_norm(pj[:, base:base + HEAD].astype(F32))
        keys, _ = head_norm(pj[:, base + HEAD:base + 2 * HEAD].astype(F32))
        qb[h] = (query * qg_ref[...]).astype(BF)
        kb[h] = (keys * kg_ref[...]).astype(BF)
        scores = dot_nt(qb[h], kb[h]) * SCALE + bias[...]
        exponent = jnp.exp(scores - jnp.max(scores, axis=-1, keepdims=True))
        prob = exponent / jnp.sum(exponent, axis=-1, keepdims=True)
        probs[h] = prob
        att[:, h * HEAD:(h + 1) * HEAD] = dot(prob.astype(BF), pj[:, base + 2 * HEAD:base + 3 * HEAD]).astype(BF)

    def head_backward(h):
        base = h * 3 * HEAD
        value = pj[:, base + 2 * HEAD:base + 3 * HEAD]
        incoming = ga[:, h * HEAD:(h + 1) * HEAD]
        prob = probs[h]
        gp[:, base + 2 * HEAD:base + 3 * HEAD] = dot_tn(prob.astype(BF), incoming).astype(BF)
        grad_probs = dot_nt(incoming, value)
        grad_scores = (prob * (grad_probs - jnp.sum(prob * grad_probs, axis=-1, keepdims=True)) * SCALE).astype(BF)
        query, query_inv = head_norm(pj[:, base:base + HEAD].astype(F32))
        keys, key_inv = head_norm(pj[:, base + HEAD:base + 2 * HEAD].astype(F32))
        grad_qn = dot(grad_scores, kb[h])
        grad_kn = dot_tn(grad_scores, qb[h])
        gp[:, base:base + HEAD] = head_norm_back(grad_qn, query, query_inv, qg_ref[...]).astype(BF)
        gp[:, base + HEAD:base + 2 * HEAD] = head_norm_back(grad_kn, keys, key_inv, kg_ref[...]).astype(BF)

    def make_terms(group, left, weights, terms):
        def some(places):
            blocks = []
            for dy, dz in places:
                block = ((y + dy) % RING) * RING + (z + dz) % RING
                blocks.append(weights[pl.ds(pl.multiple_of(block * FEAT, 128), FEAT), :])
            value = dot_nt(left[...], jnp.concatenate(blocks, axis=0)).astype(BF)
            for i, (dy, dz) in enumerate(places):
                terms[:, pl.ds((dy * RING + dz) * FEAT, FEAT)] = value[:, i * FEAT:(i + 1) * FEAT]

        if group == 0:
            some([(2, 1), (2, 2), (2, 3)])
            some([(1, 2), (3, 2)])
        elif group == 1:
            some([(1, 1), (1, 3)])
            some([(3, 1), (3, 3)])
        else:
            some([(0, 1), (0, 2), (0, 3)])
            some([(1, 0), (2, 0), (3, 0), (0, 0)])

    project(0)
    project(1)
    gather_g.forward2(1)
    project(2)
    head_forward(0)
    gather_g.forward2(-1)
    head_forward(1)
    load_o.wait()
    make_terms(0, att, wo, term)
    gather_g.forward2(2)
    scatter_p.send(2)
    make_terms(1, att, wo, term)
    scatter_p.send(1)
    scatter_p.send(3)
    make_terms(2, att, wo, term)
    scatter_p.send(0)
    gather_g.finish()

    def grad_attended():
        ga[...] = dot(gf[...], wo[...]).astype(BF)

    grad_o.send(2)
    grad_o.send(1)
    grad_o.send(3)
    grad_attended()
    grad_o.add(2)
    head_backward(0)
    head_backward(1)
    grad_q.send(2)
    grad_o.add(1)
    grad_o.add(3)
    scatter_p.pass_on(2)
    grad_q.send(1)
    grad_q.add(2)
    scatter_p.pass_on(1)
    grad_q.send(3)
    grad_o.ring.pass_on()
    grad_q.add(1)
    scatter_p.pass_on(3)
    grad_q.add(3)
    scatter_p.pass_on(0)
    grad_o.send(0)
    scatter_p.collect(2)
    grad_o.add(0)
    settle(gather_g.copies())
    make_terms(0, gp, wq, gf)
    scatter_b.send(2)
    scatter_p.collect(1)
    scatter_p.collect(3)
    make_terms(1, gp, wq, gf)
    scatter_b.send(1)
    scatter_b.send(3)
    scatter_p.last_pass()
    make_terms(2, gp, wq, gf)
    scatter_b.send(0)
    scatter_p.collect(0)
    scatter_b.pass_on(2)
    for h in (0, 1):
        rows = pl.ds(h * HALF, HALF)
        live = lax.broadcasted_iota(jnp.int32, (HALF, FEAT), 0) + h * HALF < total_rows
        value = own_x[rows, :].astype(F32) + scatter_p.result(h)
        block_ref[rows, :] = jnp.where(live, value, 0.0).astype(BF)
    saved(pltpu.make_async_copy(block_ref, block_hbm, lsem.at[2]))
    grad_q.ring.pass_on()
    scatter_b.pass_on(1)
    grad_q.send(0)
    scatter_b.pass_on(3)
    grad_o.begin_finish()
    grad_o.finish(out_hbm, (3, 14))
    scatter_b.pass_on(0)
    scatter_b.collect(2)
    grad_q.add(0)
    scatter_b.collect(1)
    scatter_b.collect(3)
    scatter_b.last_pass()
    scatter_b.collect(0)
    for h in (0, 1):
        rows = pl.ds(h * HALF, HALF)
        own_g[rows, :] = (own_g[rows, :].astype(F32) + scatter_b.result(h)).astype(BF)
    og2[...] = dot_tn(pack[...], own_g[...]).astype(BF)
    for copy in swap_g:
        start(copy)
    ar2[here, :] = og2[here, :]
    grad_q.begin_finish()
    grad_q.finish(qkv_hbm, (4, 15))
    for copy in swap_g:
        copy.wait_recv()
    pgrad_ref[...] = dot(sel_t[...], ar2[...]).astype(BF)
    saved(pltpu.make_async_copy(pgrad_ref, pgrad_hbm, lsem.at[5]))
    grad_q.close()
    grad_o.close()
    settle(list(sent.values()))
    for copy in saves:
        copy.wait()


def hand_over(*refs):
    inputs, outputs, held, sems = refs[:4], refs[4:8], refs[8:12], refs[12]
    pairs = []
    for source, target, stage in zip(inputs, outputs, held):
        pieces = max(1, source.shape[0] * source.shape[1] // (384 * 768))
        step = source.shape[0] // pieces
        for p in range(pieces):
            at = pl.ds(p * step, step)
            k = len(pairs)
            pairs.append((
                pltpu.make_async_copy(source.at[at], stage.at[at], sems.at[0, k]),
                pltpu.make_async_copy(stage.at[at], target.at[at], sems.at[1, k]),
            ))
    for fetch, _ in pairs:
        fetch.start()
    for fetch, store in pairs:
        fetch.wait()
        store.start()
    for _, store in pairs:
        store.wait()


def shards(
    patches, keep_index, keep_count, pack_dest, pack_offset, w_qkv, q_gain, k_gain, w_out, cotangent
):
    hbm = pl.BlockSpec(memory_space=pltpu.HBM)
    results = (
        jax.ShapeDtypeStruct((ROWS, FEAT), BF),
        jax.ShapeDtypeStruct((ROWS, FEAT), BF),
        jax.ShapeDtypeStruct((GRAD_ROWS, QKV), F32),
        jax.ShapeDtypeStruct((GRAD_ROWS, OUT), F32),
    )
    done = pl.pallas_call(
        kernel,
        out_shape=results,
        in_specs=[hbm] * 10,
        out_specs=(hbm,) * 4,
        scratch_shapes=[
            pltpu.SMEM((N_DP * N_DP,), jnp.int32),
            pltpu.SMEM((N_DP * N_DP,), jnp.int32),
            pltpu.SMEM((N_DP * N_DP,), jnp.int32),
            pltpu.VMEM((N_DP, SLOTS), jnp.int32),
            pltpu.VMEM((1, HEAD), F32),
            pltpu.VMEM((1, HEAD), F32),
            pltpu.VMEM((ROWS, FEAT), BF),
            pltpu.VMEM((ROWS, FEAT), BF),
            *(pltpu.VMEM(r.shape, r.dtype) for r in results),
            pltpu.VMEM((D, QKV), BF),
            pltpu.VMEM((D, OUT), BF),
            pltpu.VMEM((ROWS, D), BF),
            pltpu.VMEM((ROWS, D), BF),
            pltpu.VMEM((ROWS, D), BF),
            pltpu.VMEM((ROWS, QKV), BF),
            pltpu.VMEM((ROWS, QKV), BF),
            pltpu.VMEM((ROWS, OUT), BF),
            pltpu.VMEM((ROWS, OUT), BF),
            pltpu.VMEM((HEADS_DEV, ROWS, HEAD), BF),
            pltpu.VMEM((HEADS_DEV, ROWS, HEAD), BF),
            pltpu.VMEM((HEADS_DEV, ROWS, ROWS), F32),
            pltpu.VMEM((ROWS, ROWS), F32),
            pltpu.VMEM((ROWS, ROWS), BF),
            pltpu.VMEM((ROWS, ROWS), BF),
            pltpu.VMEM((ROWS, FEAT), BF),
            pltpu.VMEM((ROWS, FEAT), BF),
            pltpu.VMEM((ROWS, FEAT), BF),
            pltpu.VMEM((ROWS, FEAT), BF),
            pltpu.VMEM((ROWS, FEAT), BF),
            pltpu.VMEM((ROWS, FEAT), BF),
            pltpu.VMEM((2, RING + 1, 3 * HALF, FEAT), BF),
            pltpu.VMEM((2, RING + 1, 3 * HALF, FEAT), BF),
            pltpu.VMEM((2, GRAD_ROWS, QKV), BF),
            pltpu.VMEM((RING, GRAD_ROWS, QKV), BF),
            pltpu.VMEM((3 * GRAD_ROWS, QKV), BF),
            pltpu.VMEM((4, GRAD_ROWS, OUT), BF),
            pltpu.VMEM((RING, GRAD_ROWS, OUT), BF),
            pltpu.VMEM((3 * GRAD_ROWS, OUT), BF),
            pltpu.SemaphoreType.DMA((N_SEMS,)),
            pltpu.SemaphoreType.DMA((N_SEMS,)),
            pltpu.SemaphoreType.DMA((16,)),
        ],
        compiler_params=pltpu.CompilerParams(
            collective_id=0, has_side_effects=True, vmem_limit_bytes=63 << 20
        ),
        cost_estimate=pl.CostEstimate(flops=15_000_000_000, bytes_accessed=20_000_000, transcendentals=300_000),
        name="block",
    )(
        keep_count, pack_dest, pack_offset, keep_index, q_gain.reshape(1, HEAD), k_gain.reshape(1, HEAD),
        patches, cotangent, w_qkv, w_out,
    )
    return pl.pallas_call(
        hand_over,
        out_shape=results,
        in_specs=[hbm] * 4,
        out_specs=(hbm,) * 4,
        scratch_shapes=[
            *(pltpu.VMEM(r.shape, r.dtype) for r in results),
            pltpu.SemaphoreType.DMA((2, 8)),
        ],
        name="hand_over",
    )(*done)


def solution(mesh):
    placed = (
        P("dp", "mp"), P("dp", None), P(), P(), P(), P(None, "mp"), P(), P(), P(None, "mp"), P("dp", "mp"),
    )
    return jax.shard_map(
        shards, mesh=mesh, in_specs=placed, out_specs=(P("dp", "mp"),) * 4, check_vma=False,
    )
```
